128 devices in a mesh: seq: 16 (over y_hi, z, core), tp: 8 (over x, y_lo).
Axes of the slice: x: 4, y: 4 (y_hi: 2, y_lo: 2; y = y_hi * 2 + y_lo), z: 4, core: 2. Of those that a mesh axis runs over, the one named last changes fastest.
Arguments:
- cond_hidden: bfloat16 [2048, 10240], P('seq', 'tp'), may hold values from -6 to 6
- cond_down: bfloat16 [10240, 3584], P('tp'), may hold values from -0.0625 to 0.0625
- cond_resid: bfloat16 [2048, 3584], P('seq', 'tp'), may hold values from -6 to 6
- cond_gain: float32 [3584], replicated, may hold values from 0.25 to 1.75
- text_proj: bfloat16 [3584, 3072], P(None, 'tp'), may hold values from -0.09375 to 0.09375
- image_states: bfloat16 [8192, 3072], P('seq', 'tp'), may hold values from -6 to 6
- image_mod: float32 [4, 3072], replicated, may hold values from -6 to 6
- text_mod: float32 [4, 3072], replicated, may hold values from -6 to 6
- query_gain: float32 [128], replicated, may hold values from 1 to 2.2
- key_gain: float32 [128], replicated, may hold values from 1 to 2.2
- image_qkv: bfloat16 [3072, 3, 3072], P('seq', None, 'tp'), may hold values from -0.109375 to 0.109375
- text_qkv: bfloat16 [3072, 3, 3072], P('seq', None, 'tp'), may hold values from -0.109375 to 0.109375
- image_out: bfloat16 [3072, 3072], P('tp', 'seq'), may hold values from -0.109375 to 0.109375
- text_out: bfloat16 [3072, 3072], P('tp', 'seq'), may hold values from -0.109375 to 0.109375
- cond_pos: int32 [2048], P('seq'), may hold values from 0 to 16383
- image_cache: bfloat16 [8192, 3072], P('seq', 'tp'), may hold values from -6 to 6
- text_cache: bfloat16 [2048, 3072], P('seq', 'tp'), may hold values from -6 to 6
Outputs:
- image_next: bfloat16 [8192, 3072], P('seq', 'tp')
- text_next: bfloat16 [2048, 3072], P('seq', 'tp')
The draws below stay inside these ranges and needn't reach their ends.
All inputs are finite; a program needn't handle non-finite values.
Results may differ from the reference program's by a relative error of at most 0.035.
Values may be sent and summed in bfloat16 or wider, within the bound.
No kernel may reach another device: no remote copies, remote signals or barrier semaphores. Data moves between devices by JAX's collectives and lax.ppermute only.
A program may use at most 256 MiB of HBM per device.

```python
import math
import jax
import jax.numpy as jnp
from jax import lax

HD = 128
D = 3072
DE = 3584
FFE = 10240
IMAGE = 8192
COND = 2048
N_TP = 8


def touch_ends(entries, key, low, high):
    longest = entries.shape.index(max(entries.shape))
    spots = []
    for shift in (0, 1):
        where = [jax.random.randint(jax.random.fold_in(key, axis), (), 0, length) for axis, length in enumerate(entries.shape)]
        where[longest] = (where[longest] + shift) % entries.shape[longest]
        spots.append(tuple(where))
    return entries.at[spots[0]].set(low).at[spots[1]].set(high)


def steps_of(stream_key, shape, cuts, smallest, high):
    factor_of = 1.0
    for position, shards_of in cuts:
        draws = jax.random.uniform(jax.random.fold_in(jax.random.fold_in(stream_key, 6), position), (shards_of,), jnp.float32, smallest / len(cuts), high / len(cuts))
        factor_of = factor_of * jnp.repeat(jnp.exp(draws), shape[position] // shards_of).reshape((-1,) + (1,) * (len(shape) - 1 - position))
    return factor_of


def scatter_about(key, dims, scale, bound, pieces=(), kind=jnp.bfloat16):
    array = scale * jax.random.normal(key, dims, jnp.float32)
    if pieces:
        array = array * steps_of(key, dims, pieces, -0.22, 0.18)
    return jnp.clip(array, -bound, bound).astype(kind)


def setup_inputs(seed: int = 0) -> dict:
    key_of = jax.random.split(jax.random.key(seed), 18)
    return {
        "cond_hidden": scatter_about(key_of[0], (COND, FFE), 1.0, 6.0, ((0, 16), (1, 8))),
        "cond_down": scatter_about(key_of[1], (FFE, DE), FFE ** -0.5, 0.0625, ((0, 8),)),
        "cond_resid": scatter_about(key_of[2], (COND, DE), 1.0, 6.0, ((0, 16), (1, 8))),
        "cond_gain": jnp.clip(1.0 + 0.15 * jax.random.normal(key_of[3], (DE,), jnp.float32), 0.25, 1.75),
        "text_proj": scatter_about(key_of[4], (DE, D), DE ** -0.5, 0.09375, ((1, 8),)),
        "image_states": scatter_about(key_of[5], (IMAGE, D), 1.0, 6.0, ((0, 16), (1, 8))),
        "image_mod": scatter_about(key_of[6], (4, D), 1.0, 6.0, (), jnp.float32),
        "text_mod": scatter_about(key_of[7], (4, D), 1.0, 6.0, (), jnp.float32),
        "query_gain": jnp.clip(jnp.exp(jax.random.uniform(key_of[8], (HD,), jnp.float32, math.log(1.0), math.log(2.2))), 1.0, 2.2),
        "key_gain": jnp.clip(jnp.exp(jax.random.uniform(key_of[9], (HD,), jnp.float32, math.log(1.0), math.log(2.2))), 1.0, 2.2),
        "image_qkv": scatter_about(key_of[10], (D, 3, D), D ** -0.5, 0.109375, ((0, 16), (2, 8))),
        "text_qkv": scatter_about(key_of[11], (D, 3, D), D ** -0.5, 0.109375, ((0, 16), (2, 8))),
        "image_out": scatter_about(key_of[12], (D, D), D ** -0.5, 0.109375, ((0, 8), (1, 16))),
        "text_out": scatter_about(key_of[13], (D, D), D ** -0.5, 0.109375, ((0, 8), (1, 16))),
        "cond_pos": touch_ends(jax.random.randint(key_of[14], (COND,), 0, 4 * COND + IMAGE), jax.random.fold_in(key_of[14], 1), 0, (4 * COND + IMAGE) - 1).astype(jnp.int32),
        "image_cache": scatter_about(key_of[15], (IMAGE, D), 1.0, 6.0, ((0, 16), (1, 8))),
        "text_cache": scatter_about(key_of[16], (COND, D), 1.0, 6.0, ((0, 16), (1, 8))),
    }


EPS = 1e-06

def modulate(states, modulation):
    values = states.astype(jnp.float32)
    center = lax.optimization_barrier(jnp.mean(values, axis=-1, keepdims=True))
    shifted = values - center
    spread = lax.optimization_barrier(jnp.mean(shifted * shifted, axis=-1, keepdims=True))
    normed = shifted * lax.rsqrt(spread + EPS)
    return (normed * (1.0 + modulation[1]) + modulation[0]).astype(jnp.bfloat16)

def rotate(values, positions):
    half_size = values.shape[-1] // 2
    freqs = 10000.0 ** (-(jnp.arange(half_size, dtype=jnp.float32) * 2.0) / values.shape[-1])
    angles = positions[:, None] * freqs[None, :]
    cosine = jnp.cos(angles)[:, None, :]
    sine = jnp.sin(angles)[:, None, :]
    first = values[..., :half_size]
    second = values[..., half_size:]
    return jnp.concatenate([first * cosine - second * sine, second * cosine + first * sine], axis=-1)

def prepare(flat, gain, positions, head_size):
    shaped = flat.reshape(flat.shape[0], -1, head_size)
    meansq = lax.optimization_barrier(jnp.mean(shaped * shaped, axis=-1, keepdims=True))
    normed = shaped * lax.rsqrt(meansq + EPS) * gain
    return rotate(normed, positions).astype(jnp.bfloat16)

def group_sum(attended_rows, out_weight):
    group_width = attended_rows.shape[1] // N_TP

    def add_group(group, total):
        offset = (group * group_width).astype(jnp.int32)
        left = lax.dynamic_slice_in_dim(attended_rows, offset, group_width, 1)
        right = lax.dynamic_slice_in_dim(out_weight, offset, group_width, 0)
        rounded = lax.optimization_barrier(jnp.dot(left, right, preferred_element_type=jnp.float32).astype(jnp.bfloat16))
        return total + rounded.astype(jnp.float32)
    start_total = jnp.zeros((attended_rows.shape[0], out_weight.shape[1]), jnp.float32)
    return lax.fori_loop(jnp.int32(0), jnp.int32(N_TP), add_group, start_total)

def reference(cond_hidden, cond_down, cond_resid, cond_gain, text_proj, image_states, image_mod, text_mod, query_gain, key_gain, image_qkv, text_qkv, image_out, text_out, cond_pos, image_cache, text_cache):
    summed = cond_resid.astype(jnp.float32) + jnp.dot(cond_hidden, cond_down, preferred_element_type=jnp.float32)
    rounded = lax.optimization_barrier(summed.astype(jnp.bfloat16))
    cond_state = rounded.astype(jnp.float32)
    cond_normed = (cond_state * lax.rsqrt(lax.optimization_barrier(jnp.mean(cond_state * cond_state, axis=-1, keepdims=True)) + EPS) * cond_gain).astype(jnp.bfloat16)
    text_states = jnp.dot(cond_normed, text_proj, preferred_element_type=jnp.float32).astype(jnp.bfloat16)
    width = image_states.shape[1]
    head_size = query_gain.shape[0]
    image_rows = image_states.shape[0]
    image_proj = jnp.dot(modulate(image_states, image_mod), image_qkv.reshape(width, 3 * width), preferred_element_type=jnp.float32)
    text_projected = jnp.dot(modulate(text_states, text_mod), text_qkv.reshape(width, 3 * width), preferred_element_type=jnp.float32)
    projected = jnp.concatenate([image_proj, text_projected], axis=0)
    positions = jnp.concatenate([jnp.arange(image_rows).astype(jnp.float32), cond_pos.astype(jnp.float32)])
    queries = prepare(projected[:, :width], query_gain, positions, head_size)
    keys = prepare(projected[:, width:2 * width], key_gain, positions, head_size)
    values = projected[:, 2 * width:].astype(jnp.bfloat16).reshape(projected.shape[0], -1, head_size)
    scaling = 1.0 / jnp.sqrt(jnp.float32(head_size))

    def one_head(operands):
        query_head, key_head, value_head = operands
        scores = jnp.dot(query_head, key_head.T, preferred_element_type=jnp.float32) * scaling
        weights = jnp.exp(scores)
        totals = lax.optimization_barrier(jnp.sum(weights, axis=-1))
        mixed = jnp.dot(weights.astype(jnp.bfloat16), value_head, preferred_element_type=jnp.float32)
        return (mixed / totals[:, None]).astype(jnp.bfloat16)
    heads_first = lax.map(one_head, (jnp.transpose(queries, (1, 0, 2)), jnp.transpose(keys, (1, 0, 2)), jnp.transpose(values, (1, 0, 2))))
    attended = jnp.transpose(heads_first, (1, 0, 2)).reshape(projected.shape[0], width)
    image_branch = group_sum(attended[:image_rows], image_out)
    text_branch = group_sum(attended[image_rows:], text_out)
    image_next = (image_states.astype(jnp.float32) + image_mod[2] * image_branch + image_mod[3] * image_cache.astype(jnp.float32)).astype(jnp.bfloat16)
    text_next = (text_states.astype(jnp.float32) + text_mod[2] * text_branch + text_mod[3] * text_cache.astype(jnp.float32)).astype(jnp.bfloat16)
    return (image_next, text_next)
```

```python
import functools
import math

import jax
import jax.numpy as jnp
from jax import lax
from jax.experimental import pallas as pl
from jax.experimental.pallas import tpu as pltpu
from jax.sharding import Mesh, PartitionSpec as P

EPS = 1e-06
HD = 128
AXES = ("yh", "z", "c", "x", "yl")
SEQ = ("yh", "z", "c")
TP = ("x", "yl")
BF = jnp.bfloat16
F32 = jnp.float32


def shift(value, axis, step):
    size = lax.axis_size(axis)
    return lax.ppermute(value, axis, [(k, (k + step) % size) for k in range(size)])


def ring(value, axis, dim):
    left = shift(value, axis, 1)
    right = shift(value, axis, -1)
    half = value.shape[dim] // 2
    top = shift(lax.slice_in_dim(left, 0, half, axis=dim), axis, 1)
    bottom = shift(lax.slice_in_dim(right, half, 2 * half, axis=dim), axis, -1)
    return [(value, None, 0), (left, None, 3), (right, None, 1), (top, 0, 2), (bottom, 1, 2)]


def gather(value, pair, axis, dim):
    other = shift(value, pair, 1)
    near = [(b, h, 0, d) for b, h, d in ring(value, axis, dim)]
    return near + [(b, h, 1, d) for b, h, d in ring(other, axis, dim)]


def with_core(pieces):
    own = [(b, h, 0, p, d) for b, h, p, d in pieces]
    return own + [(shift(b, "c", 1), h, 1, p, d) for b, h, p, d in pieces]


def tp_places(pieces):
    x, yl = lax.axis_index("x"), lax.axis_index("yl")
    return [((x + d) % 4) * 2 + (yl + p) % 2 for _, _, p, d in pieces]


def seq_places(pieces):
    yh, z, c = lax.axis_index("yh"), lax.axis_index("z"), lax.axis_index("c")
    return [((yh + p) % 2) * 8 + ((z + d) % 4) * 2 + (c + k) % 2 for _, _, k, p, d in pieces]


def table(places):
    return jnp.stack([jnp.asarray(p, jnp.int32) for p in places])


def params(mib=48):
    return pltpu.CompilerParams(vmem_limit_bytes=mib * 1024 * 1024)


ANY = pl.BlockSpec(memory_space=pl.ANY)
VMEM = pl.BlockSpec(memory_space=pltpu.VMEM)
SMEM = pl.BlockSpec(memory_space=pltpu.SMEM)


def text_kernel(places, halves, place_ref, gain_ref, proj_ref, *refs):
    count = len(halves)
    pieces, out_ref = refs[:count], refs[count]
    state, sems = refs[count + 1 :]
    rows = state.shape[1]
    copies = []
    for i, half in enumerate(halves):
        dst = state.at[place_ref[i]]
        if half is not None:
            dst = dst.at[pl.ds(half * (rows // 2), rows // 2)]
        copies.append(pltpu.make_async_copy(pieces[i], dst, sems.at[i]))
        copies[-1].start()
    for copy in copies:
        copy.wait()
    parts, share = state.shape[0], state.shape[2]
    square = jnp.zeros((rows, 1), F32)
    for t in range(parts):
        block = state[t].astype(F32)
        square += jnp.sum(block * block, axis=-1, keepdims=True)
    factor = lax.rsqrt(square / (parts * share) + EPS)
    total = jnp.zeros(out_ref.shape, F32)
    for t in range(parts):
        normed = (state[t].astype(F32) * factor * gain_ref[t]).astype(BF)
        total += jnp.dot(normed, proj_ref[t], preferred_element_type=F32)
    out_ref[...] = total.astype(BF)


def text_projection(pieces, gain, proj):
    places = tp_places(pieces)
    halves = tuple(h for _, h, _, _ in pieces)
    share = pieces[0][0].shape[1]
    rows = pieces[0][0].shape[0]
    parts = proj.shape[0] // share
    return pl.pallas_call(
        functools.partial(text_kernel, None, halves),
        out_shape=jax.ShapeDtypeStruct((rows, proj.shape[1]), BF),
        in_specs=[SMEM, VMEM, VMEM] + [ANY] * len(pieces),
        out_specs=VMEM,
        scratch_shapes=[
            pltpu.VMEM((parts, rows, share), BF),
            pltpu.SemaphoreType.DMA((len(pieces),)),
        ],
        compiler_params=params(),
        name="text_projection",
    )(
        table(places),
        gain.reshape(parts, 1, share),
        proj.reshape(parts, share, proj.shape[1]),
        *[p[0] for p in pieces],
    )


def qkv_kernel(a_halves, w_halves, place_ref, mod_ref, cos_ref, sin_ref, gain_ref, *refs):
    na, nw = len(a_halves), len(w_halves)
    a_pieces, w_pieces = refs[:na], refs[na : na + nw]
    q_ref, kv_ref = refs[na + nw : na + nw + 2]
    states, modded, weight, sems = refs[na + nw + 2 :]
    parts, rows, share = states.shape
    width = parts * share
    depth = width // 16
    a_copies, w_copies = [], []
    for i, half in enumerate(a_halves):
        dst = states.at[place_ref[i]]
        if half is not None:
            dst = dst.at[pl.ds(half * (rows // 2), rows // 2)]
        a_copies.append(pltpu.make_async_copy(a_pieces[i], dst, sems.at[i]))
    for i, half in enumerate(w_halves):
        start, size = place_ref[na + i] * depth, depth
        if half is not None:
            start, size = start + half * (depth // 2), depth // 2
        start = pl.multiple_of(start, 32)
        dst = weight.at[:, pl.ds(start, size), :]
        w_copies.append(pltpu.make_async_copy(w_pieces[i], dst, sems.at[na + i]))
    for copy in a_copies + w_copies:
        copy.start()
    for copy in a_copies:
        copy.wait()

    tile = 64

    @pl.loop(0, rows // tile)
    def _(step):
        here = pl.ds(pl.multiple_of(step * tile, tile), tile)
        total = jnp.zeros((tile, share), F32)
        for t in range(parts):
            total += states[t, here, :].astype(F32)
        center = jnp.sum(total, axis=-1, keepdims=True) / width
        total = jnp.zeros((tile, share), F32)
        for t in range(parts):
            shifted = states[t, here, :].astype(F32) - center
            total += shifted * shifted
        factor = lax.rsqrt(jnp.sum(total, axis=-1, keepdims=True) / width + EPS)
        for t in range(parts):
            cols = slice(t * share, (t + 1) * share)
            shifted = states[t, here, :].astype(F32) - center
            normed = shifted * factor * (1.0 + mod_ref[1:2, cols]) + mod_ref[0:1, cols]
            modded[here, cols] = normed.astype(BF)

    for copy in w_copies:
        copy.wait()

    chunk = min(rows, 256)

    def project(here, j):
        return jnp.dot(modded[here, :], weight[j], preferred_element_type=F32)

    def prepare(flat, gain, cosine, sine):
        outs = []
        for h in range(share // HD):
            head = flat[:, h * HD : (h + 1) * HD]
            meansq = jnp.mean(head * head, axis=-1, keepdims=True)
            normed = head * lax.rsqrt(meansq + EPS) * gain
            outs.append(normed * cosine + pltpu.roll(normed, HD // 2, 1) * sine)
        return jnp.concatenate(outs, axis=1)

    @pl.loop(0, rows // chunk)
    def _(step):
        here = pl.ds(pl.multiple_of(step * chunk, chunk), chunk)
        cosine, sine = cos_ref[here, :], sin_ref[here, :]
        q = prepare(project(here, 0), gain_ref[0:1, :], cosine, sine)
        q_ref[here, :] = (q * (math.log2(math.e) / math.sqrt(HD))).astype(BF)
        kv_ref[0, here, :] = prepare(project(here, 1), gain_ref[1:2, :], cosine, sine).astype(BF)
        kv_ref[1, here, :] = project(here, 2).astype(BF)


def qkv(a_pieces, w_pieces, mod, cosine, sine, gains):
    rows, share = a_pieces[0][0].shape
    parts = 8
    width = parts * share
    places = tp_places(a_pieces) + seq_places(w_pieces)
    a_halves = tuple(p[1] for p in a_pieces)
    w_halves = tuple(p[1] for p in w_pieces)
    count = len(places)
    return pl.pallas_call(
        functools.partial(qkv_kernel, a_halves, w_halves),
        out_shape=(
            jax.ShapeDtypeStruct((rows, share), BF),
            jax.ShapeDtypeStruct((2, rows, share), BF),
        ),
        in_specs=[SMEM, VMEM, VMEM, VMEM, VMEM] + [ANY] * count,
        out_specs=(VMEM, VMEM),
        scratch_shapes=[
            pltpu.VMEM((parts, rows, share), BF),
            pltpu.VMEM((rows, width), BF),
            pltpu.VMEM((3, width, share), BF),
            pltpu.SemaphoreType.DMA((count,)),
        ],
        compiler_params=params(),
        name="qkv",
    )(table(places), mod, cosine, sine, gains, *[p[0] for p in a_pieces + w_pieces])


def attention_kernel(nq, k_sizes, tile, *refs):
    q_refs = refs[:nq]
    kv_refs = refs[nq : nq + len(k_sizes)]
    out_refs = refs[nq + len(k_sizes) : 2 * nq + len(k_sizes)]
    tot_refs = refs[2 * nq + len(k_sizes) : 3 * nq + len(k_sizes)]
    keys, values = refs[3 * nq + len(k_sizes) :]
    head = pl.program_id(0)
    at = 0
    for ref, size in zip(kv_refs, k_sizes):
        keys[at : at + size, :] = ref[0]
        values[at : at + size, 0:HD] = ref[1]
        at += size

    @pl.when(head == 0)
    def _():
        values[:, HD:] = jnp.ones((values.shape[0], HD), BF)

    lane = lax.broadcasted_iota(jnp.int32, (tile, HD), 1)
    for q_ref, out_ref, tot_ref in zip(q_refs, out_refs, tot_refs):

        @pl.loop(0, q_ref.shape[0] // tile)
        def _(step):
            here = pl.ds(pl.multiple_of(step * tile, tile), tile)
            q = q_ref[here, :]
            total = jnp.zeros((tile, 2 * HD), F32)
            block = 512
            for start in range(0, keys.shape[0], block):
                stop = min(start + block, keys.shape[0])
                scores = lax.dot_general(
                    q, keys[start:stop, :], (((1,), (1,)), ((), ())), preferred_element_type=F32
                )
                probs = jnp.exp2(scores).astype(BF)
                total += jnp.dot(probs, values[start:stop, :], preferred_element_type=F32)
            out_ref[here, :] = total[:, :HD]
            before = jnp.where(head == 0, 0.0, tot_ref[here, :])
            tot_ref[here, :] = jnp.where(lane == head, total[:, HD:], before)


def attention(queries, kvs):
    heads = queries[0].shape[1] // HD
    k_sizes = tuple(kv.shape[1] for kv in kvs)
    total = sum(k_sizes)
    nq = len(queries)
    tile = 128
    sizes = [q.shape[0] for q in queries]
    outs = pl.pallas_call(
        functools.partial(attention_kernel, nq, k_sizes, tile),
        grid=(heads,),
        out_shape=[jax.ShapeDtypeStruct((n, heads * HD), F32) for n in sizes]
        + [jax.ShapeDtypeStruct((n, HD), F32) for n in sizes],
        in_specs=[pl.BlockSpec((n, HD), lambda h: (0, h)) for n in sizes]
        + [pl.BlockSpec((2, n, HD), lambda h: (0, 0, h)) for n in k_sizes],
        out_specs=[pl.BlockSpec((n, HD), lambda h: (0, h)) for n in sizes]
        + [pl.BlockSpec((n, HD), lambda h: (0, 0)) for n in sizes],
        scratch_shapes=[pltpu.VMEM((total, HD), BF), pltpu.VMEM((total, 2 * HD), BF)],
        compiler_params=params(),
        name="attention",
    )(*queries, *kvs)
    return outs[:nq], outs[nq:]


def out_kernel(w_halves, place_ref, num_ref, tot_ref, *refs):
    nw = len(w_halves)
    w_pieces = refs[:nw]
    out_ref = refs[nw]
    weight, attended, sems = refs[nw + 1 :]
    share = num_ref.shape[1]
    depth = share // 2
    copies = []
    for i, half in enumerate(w_halves):
        start, size = place_ref[i] * depth, depth
        if half is not None:
            start, size = start + half * (depth // 2), depth // 2
        start = pl.multiple_of(start, 32)
        dst = weight.at[:, pl.ds(start, size), :]
        copies.append(pltpu.make_async_copy(w_pieces[i], dst, sems.at[i]))
        copies[-1].start()
    for h in range(share // HD):
        cols = slice(h * HD, (h + 1) * HD)
        attended[:, cols] = (num_ref[:, cols] / tot_ref[:, h : h + 1]).astype(BF)
    for copy in copies:
        copy.wait()
    image_rows = 512
    for t in range(out_ref.shape[0]):
        for s, rows in ((0, slice(0, image_rows)), (1, slice(image_rows, None))):
            out_ref[t, rows, :] = lax.dot_general(
                attended[rows, :],
                weight[s, t * share : (t + 1) * share, :],
                (((1,), (1,)), ((), ())),
                preferred_element_type=F32,
            ).astype(BF)


def out_projection(num, tot, pieces):
    rows, share = num.shape
    halves = tuple(p[1] for p in pieces)
    return pl.pallas_call(
        functools.partial(out_kernel, halves),
        out_shape=jax.ShapeDtypeStruct((8, rows, share), BF),
        in_specs=[SMEM, VMEM, VMEM] + [ANY] * len(pieces),
        out_specs=VMEM,
        scratch_shapes=[
            pltpu.VMEM((2, 8 * share, share), BF),
            pltpu.VMEM((rows, share), BF),
            pltpu.SemaphoreType.DMA((len(pieces),)),
        ],
        compiler_params=params(),
        name="out_projection",
    )(table(seq_places(pieces)), num, tot, *[p[0] for p in pieces])


def angles_of(positions):
    freqs = 10000.0 ** (-(jnp.arange(HD // 2, dtype=F32) * 2.0) / HD)
    angles = positions[:, None] * freqs[None, :]
    cosine, sine = jnp.cos(angles), jnp.sin(angles)
    return jnp.concatenate([cosine, cosine], axis=1), jnp.concatenate([-sine, sine], axis=1)


def shards(
    cond_hidden,
    cond_down,
    cond_resid,
    cond_gain,
    text_proj,
    image_states,
    image_mod,
    text_mod,
    query_gain,
    key_gain,
    image_qkv,
    text_qkv,
    image_out,
    text_out,
    cond_pos,
    image_cache,
    text_cache,
):
    seq_index = lax.axis_index(SEQ)
    tp_index = lax.axis_index(TP)
    image_rows, share = image_states.shape
    text_rows = cond_hidden.shape[0]

    image_w = with_core(gather(jnp.transpose(image_qkv, (1, 0, 2)), "yh", "z", 1))
    image_a = gather(image_states, "yl", "x", 0)
    text_w = with_core(gather(jnp.transpose(text_qkv, (1, 0, 2)), "yh", "z", 1))
    out_w = with_core(
        gather(jnp.stack([jnp.transpose(image_out), jnp.transpose(text_out)]), "yh", "z", 1)
    )

    partial_value = jnp.dot(cond_hidden, cond_down, preferred_element_type=F32).astype(BF)
    enc_share = cond_down.shape[1] // 8
    sent = jnp.transpose(partial_value.reshape(text_rows, 8, enc_share), (1, 0, 2))
    got = lax.all_to_all(sent, TP, split_axis=0, concat_axis=0, tiled=True)
    cond_state = (jnp.sum(got.astype(F32), axis=0) + cond_resid.astype(F32)).astype(BF)
    text_states = text_projection(gather(cond_state, "yl", "x", 0), cond_gain, text_proj)
    text_a = gather(text_states, "yl", "x", 0)

    gains = jnp.stack([query_gain, key_gain])
    image_pos = (seq_index * image_rows + jnp.arange(image_rows)).astype(F32)
    image_q, image_kv = qkv(image_a, image_w, image_mod, *angles_of(image_pos), gains)
    text_q, text_kv = qkv(text_a, text_w, text_mod, *angles_of(cond_pos.astype(F32)), gains)

    def groups(value):
        core = shift(value, "c", 1)
        pair = shift(value, "yh", 1)
        return [value, core, pair, shift(pair, "c", 1)]

    queries = [v for pair in zip(groups(image_q), groups(text_q)) for v in pair]
    kvs = [b for b, _, _ in ring(image_kv, "z", 1)] + [b for b, _, _ in ring(text_kv, "z", 1)]
    nums, tots = attention(queries, kvs)

    def whole(group):
        i = 2 * group
        top = jnp.concatenate([nums[i], tots[i]], axis=1)
        return jnp.concatenate([top, jnp.concatenate([nums[i + 1], tots[i + 1]], axis=1)], axis=0)

    far = whole(2) + shift(whole(3), "c", 1)
    near = whole(0) + shift(whole(1), "c", 1)
    far_tot = far[:, share:]
    high = far_tot.astype(BF)
    low = (far_tot - high.astype(F32)).astype(BF)
    mixed = jnp.concatenate([far[:, :share].astype(BF), high[:, :64], low[:, :64]], axis=1)
    back = shift(mixed, "yh", 1).astype(F32)
    num = near[:, :share] + back[:, :share]
    tot = near[:, share : share + 64] + back[:, share : share + 64] + back[:, share + 64 :]

    parts = out_projection(num, tot, out_w)
    got = lax.all_to_all(parts, TP, split_axis=0, concat_axis=0, tiled=True)
    branch = jnp.sum(got.astype(F32), axis=0)

    def finish(states, mod, rows, cache):
        gates = lax.dynamic_slice_in_dim(mod, tp_index * share, share, 1)
        return (
            states.astype(F32) + gates[2] * branch[rows] + gates[3] * cache.astype(F32)
        ).astype(BF)

    return (
        finish(image_states, image_mod, slice(0, image_rows), image_cache),
        finish(text_states, text_mod, slice(image_rows, None), text_cache),
    )


def solution(mesh):
    fine = Mesh(mesh.devices.reshape(2, 4, 2, 4, 2), AXES)
    return jax.shard_map(
        shards,
        mesh=fine,
        in_specs=(
            P(SEQ, TP),
            P(TP, None),
            P(SEQ, TP),
            P(),
            P(None, TP),
            P(SEQ, TP),
            P(),
            P(),
            P(),
            P(),
            P(SEQ, None, TP),
            P(SEQ, None, TP),
            P(TP, SEQ),
            P(TP, SEQ),
            P(SEQ),
            P(SEQ, TP),
            P(SEQ, TP),
        ),
        out_specs=(P(SEQ, TP), P(SEQ, TP)),
        check_vma=False,
    )
```

```python
import functools
import math

import jax
import jax.numpy as jnp
from jax import lax
from jax.experimental import pallas as pl
from jax.experimental.pallas import tpu as pltpu
from jax.sharding import Mesh, PartitionSpec as P

EPS = 1e-06
HD = 128
AXES = ("yh", "z", "c", "x", "yl")
SEQ = ("yh", "z", "c")
TP = ("x", "yl")
BF = jnp.bfloat16
F32 = jnp.float32


def shift(value, axis, step):
    size = lax.axis_size(axis)
    return lax.ppermute(value, axis, [(k, (k + step) % size) for k in range(size)])


def near(value, axis):
    return shift(value, axis, 1), shift(value, axis, -1)


def far(left, right, axis, dim):
    half = left.shape[dim] // 2
    top = shift(lax.slice_in_dim(left, 0, half, axis=dim), axis, 1)
    bottom = shift(lax.slice_in_dim(right, half, 2 * half, axis=dim), axis, -1)
    return top, bottom


def spread(value, axes):
    count = lax.axis_size(axes)
    copies = jnp.broadcast_to(value[None], (count,) + value.shape)
    return lax.all_to_all(copies, axes, split_axis=0, concat_axis=0, tiled=True)


def paired(value, pair):
    return jnp.stack([value, shift(value, pair, 1)])


def table(places):
    return jnp.stack([jnp.asarray(p, jnp.int32) for p in places])


def params(mib=48):
    return pltpu.CompilerParams(vmem_limit_bytes=mib * 1024 * 1024)


ANY = pl.BlockSpec(memory_space=pl.ANY)
VMEM = pl.BlockSpec(memory_space=pltpu.VMEM)
SMEM = pl.BlockSpec(memory_space=pltpu.SMEM)


def text_kernel(state_ref, gain_ref, proj_ref, out_ref):
    parts, rows, share = state_ref.shape
    square = jnp.zeros((rows, 1), F32)
    for t in range(parts):
        block = state_ref[t].astype(F32)
        square += jnp.sum(block * block, axis=-1, keepdims=True)
    factor = lax.rsqrt(square / (parts * share) + EPS)
    total = jnp.zeros(out_ref.shape, F32)
    for t in range(parts):
        normed = (state_ref[t].astype(F32) * factor * gain_ref[t]).astype(BF)
        total += jnp.dot(normed, proj_ref[t], preferred_element_type=F32)
    out_ref[...] = total.astype(BF)


def text_projection(state, gain, proj):
    parts, rows, share = state.shape
    return pl.pallas_call(
        text_kernel,
        out_shape=jax.ShapeDtypeStruct((rows, proj.shape[1]), BF),
        in_specs=[VMEM] * 3,
        out_specs=VMEM,
        compiler_params=params(),
        name="text_projection",
    )(state, gain.reshape(parts, 1, share), proj.reshape(parts, share, proj.shape[1]))


def qkv_kernel(a_index, w_index, counts, place_ref, mod_ref, cos_ref, sin_ref, gain_ref, *refs):
    na, nw = len(a_index), len(w_index)
    a_arrays, w_arrays = refs[: counts[0]], refs[counts[0] : counts[0] + counts[1]]
    q_ref, kv_ref = refs[sum(counts) : sum(counts) + 2]
    states, modded, weight, sems = refs[sum(counts) + 2 :]
    parts, rows, share = states.shape
    width = parts * share
    depth = width // 16
    a_copies, w_copies = [], []
    for i, (array, index) in enumerate(a_index):
        src, dst = a_arrays[array].at[index], states.at[place_ref[i]]
        if src.shape[0] < rows:
            first = pl.multiple_of(place_ref[i] % 2 * (rows // 2), rows // 2)
            dst = states.at[place_ref[i] // 2, pl.ds(first, rows // 2)]
        a_copies.append(pltpu.make_async_copy(src, dst, sems.at[i]))
    for i, (array, index) in enumerate(w_index):
        src = w_arrays[array].at[index]
        size = src.shape[1]
        start = pl.multiple_of(place_ref[na + i] * size, size)
        dst = weight.at[:, pl.ds(start, size), :]
        w_copies.append(pltpu.make_async_copy(src, dst, sems.at[na + i]))
    for copy in a_copies + w_copies:
        copy.start()
    for copy in a_copies:
        copy.wait()

    tile = 64

    @pl.loop(0, rows // tile)
    def _(step):
        here = pl.ds(pl.multiple_of(step * tile, tile), tile)
        total = jnp.zeros((tile, share), F32)
        for t in range(parts):
            total += states[t, here, :].astype(F32)
        center = jnp.sum(total, axis=-1, keepdims=True) / width
        total = jnp.zeros((tile, share), F32)
        for t in range(parts):
            shifted = states[t, here, :].astype(F32) - center
            total += shifted * shifted
        factor = lax.rsqrt(jnp.sum(total, axis=-1, keepdims=True) / width + EPS)
        for t in range(parts):
            cols = slice(t * share, (t + 1) * share)
            shifted = states[t, here, :].astype(F32) - center
            normed = shifted * factor * (1.0 + mod_ref[1:2, cols]) + mod_ref[0:1, cols]
            modded[here, cols] = normed.astype(BF)

    for copy in w_copies:
        copy.wait()

    chunk = min(rows, 256)

    def project(here, j):
        return jnp.dot(modded[here, :], weight[j], preferred_element_type=F32)

    def prepare(flat, gain, cosine, sine):
        outs = []
        for h in range(share // HD):
            head = flat[:, h * HD : (h + 1) * HD]
            meansq = jnp.mean(head * head, axis=-1, keepdims=True)
            normed = head * lax.rsqrt(meansq + EPS) * gain
            outs.append(normed * cosine + pltpu.roll(normed, HD // 2, 1) * sine)
        return jnp.concatenate(outs, axis=1)

    @pl.loop(0, rows // chunk)
    def _(step):
        here = pl.ds(pl.multiple_of(step * chunk, chunk), chunk)
        cosine, sine = cos_ref[here, :], sin_ref[here, :]
        q = prepare(project(here, 0), gain_ref[0:1, :], cosine, sine)
        q_ref[here, :] = (q * (math.log2(math.e) / math.sqrt(HD))).astype(BF)
        kv_ref[0, here, :] = prepare(project(here, 1), gain_ref[1:2, :], cosine, sine).astype(BF)
        kv_ref[1, here, :] = project(here, 2).astype(BF)


def qkv(a_pieces, w_pieces, mod, cosine, sine, gains):
    (a_arrays, a_list), (w_arrays, w_list) = a_pieces, w_pieces
    rows, share = a_arrays[0].shape[-2:]
    parts = 8
    width = parts * share
    places = [p for _, _, p in a_list + w_list]
    a_index = tuple((a, i) for a, i, _ in a_list)
    w_index = tuple((a, i) for a, i, _ in w_list)
    counts = (len(a_arrays), len(w_arrays))
    return pl.pallas_call(
        functools.partial(qkv_kernel, a_index, w_index, counts),
        out_shape=(
            jax.ShapeDtypeStruct((rows, share), BF),
            jax.ShapeDtypeStruct((2, rows, share), BF),
        ),
        in_specs=[SMEM, VMEM, VMEM, VMEM, VMEM] + [ANY] * sum(counts),
        out_specs=(VMEM, VMEM),
        scratch_shapes=[
            pltpu.VMEM((parts, rows, share), BF),
            pltpu.VMEM((rows, width), BF),
            pltpu.VMEM((3, width, share), BF),
            pltpu.SemaphoreType.DMA((len(places),)),
        ],
        compiler_params=params(),
        name="qkv",
    )(table(places), mod, cosine, sine, gains, *a_arrays, *w_arrays)


def attention_kernel(nq, k_sizes, first, *refs):
    q_refs, refs = refs[:nq], refs[nq:]
    kv_refs, refs = refs[: len(k_sizes)], refs[len(k_sizes) :]
    before, refs = ([], refs) if first else (refs[: 2 * nq], refs[2 * nq :])
    out_refs, tot_refs = refs[:nq], refs[nq : 2 * nq]
    keys, values = refs[2 * nq :]
    head = pl.program_id(0)
    at = 0
    for ref, size in zip(kv_refs, k_sizes):
        keys[at : at + size, :] = ref[0]
        values[at : at + size, 0:HD] = ref[1]
        at += size

    @pl.when(head == 0)
    def _():
        values[:, HD:] = jnp.ones((values.shape[0], HD), BF)
        for i in range(nq):
            tot_refs[i][...] = jnp.zeros(tot_refs[i].shape, F32) if first else before[nq + i][...]

    rows = q_refs[0].shape[0]
    lane = lax.broadcasted_iota(jnp.int32, (rows, HD), 1)
    block = 256
    for i in range(nq):
        q = q_refs[i][...]
        total = jnp.zeros((rows, 2 * HD), F32)
        for start in range(0, keys.shape[0], block):
            stop = min(start + block, keys.shape[0])
            scores = lax.dot_general(
                q, keys[start:stop, :], (((1,), (1,)), ((), ())), preferred_element_type=F32
            )
            probs = jnp.exp2(scores).astype(BF)
            total += jnp.dot(probs, values[start:stop, :], preferred_element_type=F32)
        num = total[:, :HD]
        out_refs[i][...] = num if first else before[i][...] + num
        tot_refs[i][...] += jnp.where(lane == head, total[:, HD:], 0.0)


def attention(queries, kvs, before=()):
    rows, width = queries[0].shape
    k_sizes = tuple(kv.shape[1] for kv in kvs)
    total = sum(k_sizes)
    nq = len(queries)
    by_head = pl.BlockSpec((rows, HD), lambda h: (0, h))
    fixed = pl.BlockSpec((rows, HD), lambda h: (0, 0))
    sums = [by_head] * nq + [fixed] * nq
    inputs = nq + len(kvs)
    return pl.pallas_call(
        functools.partial(attention_kernel, nq, k_sizes, not before),
        grid=(width // HD,),
        out_shape=[jax.ShapeDtypeStruct((rows, width), F32)] * nq
        + [jax.ShapeDtypeStruct((rows, HD), F32)] * nq,
        in_specs=[by_head] * nq
        + [pl.BlockSpec((2, n, HD), lambda h: (0, 0, h)) for n in k_sizes]
        + (sums if before else []),
        out_specs=sums,
        input_output_aliases={inputs + i: i for i in range(2 * nq)} if before else {},
        scratch_shapes=[pltpu.VMEM((total, HD), BF), pltpu.VMEM((total, 2 * HD), BF)],
        compiler_params=params(),
        name="attention",
    )(*queries, *kvs, *before)


def out_kernel(place_ref, num_ref, tot_ref, weight_ref, x_ref, own_ref, other_ref, attended):
    rows, share = num_ref.shape
    image_rows = rows // 5 * 4
    half = rows // 2
    for h in range(share // HD):
        cols = slice(h * HD, (h + 1) * HD)
        attended[:, cols] = (num_ref[:, cols] / tot_ref[:, h : h + 1]).astype(BF)

    def product(stream, first, last, target):
        outs = [
            lax.dot_general(
                attended[first:last, :],
                weight_ref[2 * target + k, stream],
                (((1,), (1,)), ((), ())),
                preferred_element_type=F32,
            )
            for k in range(2)
        ]
        return jnp.concatenate(outs, axis=1).astype(BF)

    yl = place_ref[0]
    for x in range(x_ref.shape[0]):
        for y in range(2):
            x_ref[x, y] = product(0, 0, half, 2 * x + y)
        for ref, y in ((own_ref, yl), (other_ref, 1 - yl)):
            ref[x, : image_rows - half] = product(0, half, image_rows, 2 * x + y)
            ref[x, image_rows - half :] = product(1, image_rows, rows, 2 * x + y)


def out_projection(num, tot, weight, yl):
    rows, share = num.shape
    half = rows // 2
    return pl.pallas_call(
        out_kernel,
        out_shape=(
            jax.ShapeDtypeStruct((4, 2, half, share), BF),
            jax.ShapeDtypeStruct((4, half, share), BF),
            jax.ShapeDtypeStruct((4, half, share), BF),
        ),
        in_specs=[SMEM] + [VMEM] * 3,
        out_specs=(VMEM,) * 3,
        scratch_shapes=[pltpu.VMEM((rows, share), BF)],
        compiler_params=params(),
        name="out_projection",
    )(table([yl]), num, tot, weight)


def angles_of(positions):
    freqs = 10000.0 ** (-(jnp.arange(HD // 2, dtype=F32) * 2.0) / HD)
    angles = positions[:, None] * freqs[None, :]
    cosine, sine = jnp.cos(angles), jnp.sin(angles)
    return jnp.concatenate([cosine, cosine], axis=1), jnp.concatenate([-sine, sine], axis=1)


def shards(
    cond_hidden,
    cond_down,
    cond_resid,
    cond_gain,
    text_proj,
    image_states,
    image_mod,
    text_mod,
    query_gain,
    key_gain,
    image_qkv,
    text_qkv,
    image_out,
    text_out,
    cond_pos,
    image_cache,
    text_cache,
):
    seq_index = lax.axis_index(SEQ)
    tp_index = lax.axis_index(TP)
    image_rows, share = image_states.shape
    text_rows = cond_hidden.shape[0]

    yh, z, c, x, yl = (lax.axis_index(a) for a in AXES)
    together = lax.optimization_barrier
    text_w = lax.all_gather(jnp.transpose(text_qkv, (1, 0, 2)), SEQ)

    a_own = paired(image_states, "yl")
    w_own = paired(jnp.transpose(image_qkv, (1, 0, 2)), "yh")
    partial_value = jnp.dot(cond_hidden, cond_down, preferred_element_type=F32).astype(BF)
    enc_share = cond_down.shape[1] // 8
    sent = jnp.transpose(partial_value.reshape(text_rows, 8, enc_share), (1, 0, 2))
    sent, a_own, w_own = together((sent, a_own, w_own))

    a_left, a_right = near(a_own, "x")
    w_left, w_right = near(w_own, "z")
    got = lax.all_to_all(sent, TP, split_axis=0, concat_axis=0, tiled=True)
    cond_state = (jnp.sum(got.astype(F32), axis=0) + cond_resid.astype(F32)).astype(BF)
    cond_state, a_left, a_right = together((cond_state, a_left, a_right))

    a_top, a_bottom = far(a_left, a_right, "x", 1)
    state = spread(cond_state, TP)
    state, a_top, a_bottom, w_left, w_right = together((state, a_top, a_bottom, w_left, w_right))
    w_top, w_bottom = far(w_left, w_right, "z", 2)
    text_states = text_projection(state, cond_gain, text_proj)
    text_a = spread(text_states, TP)
    out_w = lax.all_gather(
        together((jnp.stack([jnp.transpose(image_out), jnp.transpose(text_out)]), state))[0], SEQ
    )

    w_arrays = [w_own, w_left, w_right, w_top, w_bottom]
    w_arrays += [shift(w, "c", 1) for w in w_arrays]

    gains = jnp.stack([query_gain, key_gain])
    image_pos = (seq_index * image_rows + jnp.arange(image_rows)).astype(F32)
    blocks = ((0, 0, None), (1, 3, None), (2, 1, None), (3, 2, 0), (4, 2, 1))

    def piece(place, half):
        return place if half is None else 2 * place + half

    image_q, image_kv = qkv(
        (
            [a_own, a_left, a_right, a_top, a_bottom],
            [
                (i, (p,), piece((x + d) % 4 * 2 + (yl + p) % 2, half))
                for i, d, half in blocks
                for p in range(2)
            ],
        ),
        (
            w_arrays,
            [
                (5 * k + i, (p,), piece((yh + p) % 2 * 8 + (z + d) % 4 * 2 + (c + k) % 2, half))
                for k in range(2)
                for i, d, half in blocks
                for p in range(2)
            ],
        ),
        image_mod,
        *angles_of(image_pos),
        gains,
    )
    text_q, text_kv = qkv(
        ([text_a], [(0, (t,), t) for t in range(8)]),
        ([text_w], [(0, (t,), t) for t in range(16)]),
        text_mod,
        *angles_of(cond_pos.astype(F32)),
        gains,
    )
    query = jnp.concatenate([image_q, text_q], axis=0)
    kv = jnp.concatenate([image_kv, text_kv], axis=1)

    pair_query = shift(query, "yh", 1)
    kv_left, kv_right = near(kv, "z")
    core_query = shift(query, "c", 1)
    queries = [query, core_query, pair_query, shift(pair_query, "c", 1)]
    sums = attention(queries, [kv])
    sums, kv_left, kv_right = together((sums, kv_left, kv_right))
    kv_top, kv_bottom = far(kv_left, kv_right, "z", 1)
    sums = attention(queries, [kv_left, kv_right], sums)
    sums, kv_top, kv_bottom = together((sums, kv_top, kv_bottom))
    sums = attention(queries, [kv_top, kv_bottom], sums)
    nums, tots = sums[:4], sums[4:]

    sent_num = nums[2] + shift(nums[3], "c", 1)
    sent_tot = tots[2] + shift(tots[3], "c", 1)
    high = sent_tot.astype(BF)
    low = (sent_tot - high.astype(F32)).astype(BF)
    mixed = jnp.concatenate([sent_num.astype(BF), high[:, :64], low[:, :64]], axis=1)
    back = shift(mixed, "yh", 1).astype(F32)
    num = nums[0] + shift(nums[1], "c", 1) + back[:, :share]
    tot = tots[0] + shift(tots[1], "c", 1)
    tot = tot[:, :64] + back[:, share : share + 64] + back[:, share + 64 :]

    along_x, own, other = out_projection(num, tot, out_w, yl)
    got_x = lax.all_to_all(along_x, "x", split_axis=0, concat_axis=0, tiled=True)
    got_y = shift(other, "yl", 1)
    summed_x = jnp.sum(got_x.astype(F32), axis=0)
    summed_y = (own.astype(F32) + got_y.astype(F32)).astype(BF)
    last_x = lax.all_to_all(summed_y, "x", split_axis=0, concat_axis=0, tiled=True)
    kept = lax.dynamic_index_in_dim(summed_x, yl, 0, keepdims=False)
    given = lax.dynamic_index_in_dim(summed_x, 1 - yl, 0, keepdims=False).astype(BF)
    last_y = shift(given, "yl", 1)
    branch = jnp.concatenate(
        [kept + last_y.astype(F32), jnp.sum(last_x.astype(F32), axis=0)], axis=0
    )

    def finish(states, mod, rows, cache):
        gates = lax.dynamic_slice_in_dim(mod, tp_index * share, share, 1)
        return (
            states.astype(F32) + gates[2] * branch[rows] + gates[3] * cache.astype(F32)
        ).astype(BF)

    return (
        finish(image_states, image_mod, slice(0, image_rows), image_cache),
        finish(text_states, text_mod, slice(image_rows, None), text_cache),
    )


def solution(mesh):
    fine = Mesh(mesh.devices.reshape(2, 4, 2, 4, 2), AXES)
    return jax.shard_map(
        shards,
        mesh=fine,
        in_specs=(
            P(SEQ, TP),
            P(TP, None),
            P(SEQ, TP),
            P(),
            P(None, TP),
            P(SEQ, TP),
            P(),
            P(),
            P(),
            P(),
            P(SEQ, None, TP),
            P(SEQ, None, TP),
            P(TP, SEQ),
            P(TP, SEQ),
            P(SEQ),
            P(SEQ, TP),
            P(SEQ, TP),
        ),
        out_specs=(P(SEQ, TP), P(SEQ, TP)),
        check_vma=False,
    )
```

```python
import functools
import math

import jax
import jax.numpy as jnp
from jax import lax
from jax.experimental import pallas as pl
from jax.experimental.pallas import tpu as pltpu
from jax.sharding import Mesh, PartitionSpec as P

EPS = 1e-06
HD = 128
AXES = ("yh", "z", "c", "x", "yl")
SEQ = ("yh", "z", "c")
TP = ("x", "yl")
BF = jnp.bfloat16
F32 = jnp.float32


def shift(value, axis, step):
    size = lax.axis_size(axis)
    return lax.ppermute(value, axis, [(k, (k + step) % size) for k in range(size)])


def near(value, axis):
    return shift(value, axis, 1), shift(value, axis, -1)


def spread(value, axes):
    count = lax.axis_size(axes)
    copies = jnp.broadcast_to(value[None], (count,) + value.shape)
    return lax.all_to_all(copies, axes, split_axis=0, concat_axis=0, tiled=True)


def table(places):
    return jnp.stack([jnp.asarray(p, jnp.int32) for p in places])


def params(mib=48):
    return pltpu.CompilerParams(vmem_limit_bytes=mib * 1024 * 1024)


ANY = pl.BlockSpec(memory_space=pl.ANY)
VMEM = pl.BlockSpec(memory_space=pltpu.VMEM)
SMEM = pl.BlockSpec(memory_space=pltpu.SMEM)


def text_kernel(state_ref, gain_ref, proj_ref, out_ref):
    parts, rows, share = state_ref.shape
    square = jnp.zeros((rows, 1), F32)
    for t in range(parts):
        block = state_ref[t].astype(F32)
        square += jnp.sum(block * block, axis=-1, keepdims=True)
    factor = lax.rsqrt(square / (parts * share) + EPS)
    total = jnp.zeros(out_ref.shape, F32)
    for t in range(parts):
        normed = (state_ref[t].astype(F32) * factor * gain_ref[t]).astype(BF)
        total += jnp.dot(normed, proj_ref[t], preferred_element_type=F32)
    out_ref[...] = total.astype(BF)


def text_projection(state, gain, proj):
    parts, rows, share = state.shape
    return pl.pallas_call(
        text_kernel,
        out_shape=jax.ShapeDtypeStruct((rows, proj.shape[1]), BF),
        in_specs=[VMEM] * 3,
        out_specs=VMEM,
        compiler_params=params(),
        name="text_projection",
    )(state, gain.reshape(parts, 1, share), proj.reshape(parts, share, proj.shape[1]))


def qkv_kernel(a_index, count, place_ref, mod_ref, cos_ref, sin_ref, gain_ref, text_ref, *refs):
    arrays = a_index[-1][0] + 1
    a_arrays, w_pieces, refs = refs[:arrays], refs[arrays : arrays + count], refs[arrays + count :]
    q_ref, kv_ref, states, modded, weight, sems = refs
    parts, rows, share = states.shape
    width = parts * share
    depth = width // 16
    image_rows = rows // 5 * 4
    a_copies, w_copies = [], ([], [])
    for i, (array, index) in enumerate(a_index):
        dst = states.at[place_ref[i], pl.ds(0, image_rows)]
        a_copies.append(pltpu.make_async_copy(a_arrays[array].at[index], dst, sems.at[i]))
    dst = states.at[:, pl.ds(image_rows, rows - image_rows)]
    a_copies.append(pltpu.make_async_copy(text_ref, dst, sems.at[8]))
    for stream in range(2):
        for i, piece in enumerate(w_pieces):
            start = pl.multiple_of(place_ref[8 + i] * depth, depth)
            src = piece.at[pl.ds(3 * stream, 3)]
            dst = weight.at[pl.ds(3 * stream, 3), pl.ds(start, depth), :]
            sem = sems.at[9 + count * stream + i]
            w_copies[stream].append(pltpu.make_async_copy(src, dst, sem))
    for copy in a_copies + w_copies[0] + w_copies[1]:
        copy.start()
    for copy in a_copies:
        copy.wait()

    tile = 64

    def modulate(first, last, stream):
        @pl.loop(first // tile, last // tile)
        def _(step):
            here = pl.ds(pl.multiple_of(step * tile, tile), tile)
            total = jnp.zeros((tile, share), F32)
            for t in range(parts):
                total += states[t, here, :].astype(F32)
            center = jnp.sum(total, axis=-1, keepdims=True) / width
            total = jnp.zeros((tile, share), F32)
            for t in range(parts):
                shifted = states[t, here, :].astype(F32) - center
                total += shifted * shifted
            factor = lax.rsqrt(jnp.sum(total, axis=-1, keepdims=True) / width + EPS)
            for t in range(parts):
                cols = slice(t * share, (t + 1) * share)
                shifted = states[t, here, :].astype(F32) - center
                gain = 1.0 + mod_ref[stream, 1:2, cols]
                normed = shifted * factor * gain + mod_ref[stream, 0:1, cols]
                modded[here, cols] = normed.astype(BF)

    def prepare(flat, gain, cosine, sine):
        outs = []
        for h in range(share // HD):
            head = flat[:, h * HD : (h + 1) * HD]
            meansq = jnp.mean(head * head, axis=-1, keepdims=True)
            normed = head * lax.rsqrt(meansq + EPS) * gain
            outs.append(normed * cosine + pltpu.roll(normed, HD // 2, 1) * sine)
        return jnp.concatenate(outs, axis=1)

    def project(here, stream):
        def product(j):
            return jnp.dot(modded[here, :], weight[3 * stream + j], preferred_element_type=F32)

        cosine, sine = cos_ref[here, :], sin_ref[here, :]
        q = prepare(product(0), gain_ref[0:1, :], cosine, sine)
        q_ref[here, :] = (q * (math.log2(math.e) / math.sqrt(HD))).astype(BF)
        kv_ref[0, here, :] = prepare(product(1), gain_ref[1:2, :], cosine, sine).astype(BF)
        kv_ref[1, here, :] = product(2).astype(BF)

    modulate(0, image_rows, 0)
    modulate(image_rows, rows, 1)
    for copy in w_copies[0]:
        copy.wait()
    chunk = image_rows // 2

    @pl.loop(0, 2)
    def _(step):
        project(pl.ds(pl.multiple_of(step * chunk, chunk), chunk), 0)

    for copy in w_copies[1]:
        copy.wait()
    project(pl.ds(image_rows, rows - image_rows), 1)


def qkv(a_arrays, a_index, a_places, text_a, w_pieces, w_places, mods, cosine, sine, gains):
    parts, text_rows, share = text_a.shape
    rows = a_arrays[0].shape[-2] + text_rows
    width = parts * share
    arrays, count = len(a_arrays), len(w_pieces)
    return pl.pallas_call(
        functools.partial(qkv_kernel, a_index, count),
        out_shape=(
            jax.ShapeDtypeStruct((rows, share), BF),
            jax.ShapeDtypeStruct((2, rows, share), BF),
        ),
        in_specs=[SMEM, VMEM, VMEM, VMEM, VMEM] + [ANY] * (1 + arrays + count),
        out_specs=(VMEM, VMEM),
        scratch_shapes=[
            pltpu.VMEM((parts, rows, share), BF),
            pltpu.VMEM((rows, width), BF),
            pltpu.VMEM((6, width, share), BF),
            pltpu.SemaphoreType.DMA((9 + 2 * count,)),
        ],
        compiler_params=params(),
        name="qkv",
    )(table(a_places + w_places), mods, cosine, sine, gains, text_a, *a_arrays, *w_pieces)


def attention_kernel(nq, k_sizes, first, *refs):
    nk = len(k_sizes)
    q_refs, refs = refs[:nq], refs[nq:]
    k_refs, v_refs, refs = refs[:nk], refs[nk : 2 * nk], refs[2 * nk :]
    before, refs = ([], refs) if first else (refs[: 2 * nq], refs[2 * nq :])
    out_refs, tot_refs = refs[:nq], refs[nq : 2 * nq]
    keys, values = refs[2 * nq :]
    head = pl.program_id(0)
    at = 0
    for k_ref, v_ref, size in zip(k_refs, v_refs, k_sizes):
        keys[at : at + size, :] = k_ref[0]
        values[at : at + size, 0:HD] = v_ref[0]
        at += size

    @pl.when(head == 0)
    def _():
        values[:, HD:] = jnp.ones((values.shape[0], HD), BF)
        for i in range(nq):
            tot_refs[i][...] = jnp.zeros(tot_refs[i].shape, F32) if first else before[nq + i][...]

    rows = q_refs[0].shape[0]
    lane = lax.broadcasted_iota(jnp.int32, (rows, HD), 1)
    block = 256
    for i in range(nq):
        q = q_refs[i][...]
        total = jnp.zeros((rows, 2 * HD), F32)
        for start in range(0, keys.shape[0], block):
            stop = min(start + block, keys.shape[0])
            scores = lax.dot_general(
                q, keys[start:stop, :], (((1,), (1,)), ((), ())), preferred_element_type=F32
            )
            probs = jnp.exp2(scores).astype(BF)
            total += jnp.dot(probs, values[start:stop, :], preferred_element_type=F32)
        num = total[:, :HD]
        out_refs[i][...] = num if first else before[i][...] + num
        tot_refs[i][...] += jnp.where(lane == head, total[:, HD:], 0.0)


def attention(queries, kvs, before=()):
    rows, width = queries[0].shape
    keys = [(kv[0].reshape(-1, rows, width), 0) for kv in kvs]
    values = [(kv[-1].reshape(-1, rows, width), 2 - len(kv)) for kv in kvs]
    k_sizes = (rows,) * len(kvs)
    nq = len(queries)
    by_head = pl.BlockSpec((rows, HD), lambda h: (0, h))
    fixed = pl.BlockSpec((rows, HD), lambda h: (0, 0))
    sums = [by_head] * nq + [fixed] * nq
    inputs = nq + 2 * len(kvs)
    work = nq * rows * len(kvs) * rows * width
    return pl.pallas_call(
        functools.partial(attention_kernel, nq, k_sizes, not before),
        grid=(width // HD,),
        out_shape=[jax.ShapeDtypeStruct((rows, width), F32)] * nq
        + [jax.ShapeDtypeStruct((rows, HD), F32)] * nq,
        in_specs=[by_head] * nq
        + [
            pl.BlockSpec((1, rows, HD), functools.partial(lambda i, h: (i, 0, h), i))
            for _, i in keys + values
        ]
        + (sums if before else []),
        out_specs=sums,
        input_output_aliases={inputs + i: i for i in range(2 * nq)} if before else {},
        scratch_shapes=[
            pltpu.VMEM((sum(k_sizes), HD), BF),
            pltpu.VMEM((sum(k_sizes), 2 * HD), BF),
        ],
        compiler_params=params(),
        cost_estimate=pl.CostEstimate(
            flops=8 * work, bytes_accessed=8 * nq * rows * width, transcendentals=work // HD
        ),
        name="attention",
    )(*queries, *[k for k, _ in keys + values], *before)


def combine_kernel(num_ref, other_ref, back_ref, tot_ref, other_tot_ref, out_ref):
    share = num_ref.shape[1]
    for h in range(share // HD):
        cols = slice(h * HD, (h + 1) * HD)
        lane, low = slice(share + h, share + h + 1), slice(share + 64 + h, share + 65 + h)
        num = num_ref[:, cols] + other_ref[:, cols] + back_ref[:, cols].astype(F32)
        tot = tot_ref[:, h : h + 1] + other_tot_ref[:, h : h + 1]
        tot += back_ref[:, lane].astype(F32) + back_ref[:, low].astype(F32)
        out_ref[:, cols] = (num / tot).astype(BF)


def combine(num, other, back, tot, other_tot):
    return pl.pallas_call(
        combine_kernel,
        out_shape=jax.ShapeDtypeStruct(num.shape, BF),
        in_specs=[VMEM] * 5,
        out_specs=VMEM,
        compiler_params=params(),
        name="combine",
    )(num, other, back, tot, other_tot)


def out_kernel(place_ref, own_ref, other_ref, weight_ref, out_ref, attended):
    rows, share = own_ref.shape
    image_rows = rows // 5 * 4

    @pl.when(pl.program_id(0) == 0)
    def _():
        first = place_ref[0] == 0
        attended[:, :share] = jnp.where(first, own_ref[...], other_ref[...])
        attended[:, share:] = jnp.where(first, other_ref[...], own_ref[...])

    for stream, here in ((0, slice(0, image_rows)), (1, slice(image_rows, rows))):
        halves = [weight_ref[2 * y : 2 * y + 2, stream].reshape(share, share) for y in range(2)]
        out_ref[0, here, :] = lax.dot_general(
            attended[here, :],
            jnp.concatenate(halves, axis=1),
            (((1,), (1,)), ((), ())),
            preferred_element_type=F32,
        ).astype(BF)


def out_projection(own, other, weight, yl):
    rows, share = own.shape
    whole = pl.BlockSpec((rows, share), lambda x: (0, 0))
    return pl.pallas_call(
        out_kernel,
        grid=(4,),
        out_shape=jax.ShapeDtypeStruct((4, rows, share), BF),
        in_specs=[SMEM, whole, whole]
        + [pl.BlockSpec((4,) + weight.shape[1:], lambda x: (x, 0, 0, 0))],
        out_specs=pl.BlockSpec((1, rows, share), lambda x: (x, 0, 0)),
        scratch_shapes=[pltpu.VMEM((rows, 2 * share), BF)],
        compiler_params=params(),
        name="out_projection",
    )(table([yl]), own, other, weight)


def angles_of(positions):
    freqs = 10000.0 ** (-(jnp.arange(HD // 2, dtype=F32) * 2.0) / HD)
    angles = positions[:, None] * freqs[None, :]
    cosine, sine = jnp.cos(angles), jnp.sin(angles)
    return jnp.concatenate([cosine, cosine], axis=1), jnp.concatenate([-sine, sine], axis=1)


def shards(
    cond_hidden,
    cond_down,
    cond_resid,
    cond_gain,
    text_proj,
    image_states,
    image_mod,
    text_mod,
    query_gain,
    key_gain,
    image_qkv,
    text_qkv,
    image_out,
    text_out,
    cond_pos,
    image_cache,
    text_cache,
):
    seq_index = lax.axis_index(SEQ)
    tp_index = lax.axis_index(TP)
    image_rows, share = image_states.shape
    text_rows = cond_hidden.shape[0]

    yh, z, c, x, yl = (lax.axis_index(a) for a in AXES)
    together = lax.optimization_barrier
    outs = jnp.stack([jnp.transpose(image_out), jnp.transpose(text_out)])
    weight = jnp.transpose(jnp.concatenate([image_qkv, text_qkv], axis=1), (1, 0, 2))

    turned = [
        (4 * zh + 2 * zl + y, 4 * zh + 2 * y + zl)
        for zh in range(2)
        for zl in range(2)
        for y in range(2)
    ]
    outs = lax.ppermute(outs, ("z", "yl"), turned)
    w_near = near(weight, "z")
    w_pair = shift(weight, "yh", 1)
    a_own = jnp.stack([image_states, shift(image_states, "yl", 1)])
    cond_hidden, a_own, outs = together((cond_hidden, a_own, outs))

    a_near = near(a_own, "x")
    out_w = lax.all_gather(outs, SEQ)
    partial_value = jnp.dot(cond_hidden, cond_down, preferred_element_type=F32).astype(BF)
    enc_share = cond_down.shape[1] // 8
    sent = jnp.transpose(partial_value.reshape(text_rows, 8, enc_share), (1, 0, 2))
    got = lax.all_to_all(sent, TP, split_axis=0, concat_axis=0, tiled=True)

    got, w_near, w_pair = together((got, w_near, w_pair))
    w_next = near(w_pair, "z")
    cond_state = (jnp.sum(got.astype(F32), axis=0) + cond_resid.astype(F32)).astype(BF)
    state = spread(cond_state, TP)
    state, a_near, w_near, w_next = together((state, a_near, w_near, w_next))

    text_states = text_projection(state, cond_gain, text_proj)
    text_a = spread(text_states, TP)
    a_far = (shift(a_near[0][0], "x", 1), shift(a_near[1][1], "x", -1))
    w_far = (shift(w_near[0], "z", 1), shift(w_next[1], "z", -1))
    text_a, a_far, w_far = together((text_a, a_far, w_far))

    a_arrays = [a_own, *a_near, *a_far]
    a_index = tuple((i, (p,)) for i in range(3) for p in range(2)) + ((3, ()), (4, ()))
    a_places = [
        (x + d) % 4 * 2 + (yl + p) % 2 for d, p in [(d, p) for d in (0, 3, 1, 2) for p in range(2)]
    ]
    w_arrays = [weight, *w_near, w_far[0], w_pair, *w_next, w_far[1]]
    w_arrays += [shift(w, "c", 1) for w in w_arrays]
    blocks = [(p, d) for p in range(2) for d in (0, 3, 1, 2)]

    gains = jnp.stack([query_gain, key_gain])
    image_pos = (seq_index * image_rows + jnp.arange(image_rows)).astype(F32)
    w_places = [
        (yh + p) % 2 * 8 + (z + d) % 4 * 2 + (c + k) % 2 for k in range(2) for p, d in blocks
    ]
    query, kv = qkv(
        a_arrays,
        a_index,
        a_places,
        text_a,
        w_arrays,
        w_places,
        jnp.stack([image_mod, text_mod]),
        *angles_of(jnp.concatenate([image_pos, cond_pos.astype(F32)])),
        gains,
    )
    pair_query = shift(query, "yh", 1)
    kv_left, kv_right = near(kv, "z")
    core_query = shift(query, "c", 1)
    own_queries = [query, core_query]
    own = attention(own_queries, [(kv,)])
    pair_query, own = together((pair_query, own))
    pair_queries = [pair_query, shift(pair_query, "c", 1)]
    pair = attention(pair_queries, [(kv,)])
    pair, kv_left, kv_right = together((pair, kv_left, kv_right))
    kv_far = (shift(kv_left[0], "z", 1), shift(kv_right[1], "z", -1))
    pair = attention(pair_queries, [(kv_left,), (kv_right,)], pair)
    pair, kv_far = together((pair, kv_far))
    pair = attention(pair_queries, [kv_far], pair)

    sent_num = pair[0] + shift(pair[1], "c", 1)
    sent_tot = pair[2] + shift(pair[3], "c", 1)
    high = sent_tot.astype(BF)
    low = (sent_tot - high.astype(F32)).astype(BF)
    mixed = jnp.concatenate([sent_num.astype(BF), high[:, :64], low[:, :64]], axis=1)
    mixed, own = together((mixed, own))
    back = shift(mixed, "yh", 1)
    own = attention(own_queries, [(kv_left,), (kv_right,), kv_far], own)
    back, own = together((back, own))
    attended = combine(own[0], shift(own[1], "c", 1), back, own[2], shift(own[3], "c", 1))

    parts = out_projection(attended, shift(attended, "yl", 1), out_w, yl)
    got = lax.all_to_all(parts, "x", split_axis=0, concat_axis=0, tiled=True)
    branch = jnp.sum(got.astype(F32), axis=0)

    def finish(states, mod, rows, cache):
        gates = lax.dynamic_slice_in_dim(mod, tp_index * share, share, 1)
        return (
            states.astype(F32) + gates[2] * branch[rows] + gates[3] * cache.astype(F32)
        ).astype(BF)

    return (
        finish(image_states, image_mod, slice(0, image_rows), image_cache),
        finish(text_states, text_mod, slice(image_rows, None), text_cache),
    )


def solution(mesh):
    fine = Mesh(mesh.devices.reshape(2, 4, 2, 4, 2), AXES)
    return jax.shard_map(
        shards,
        mesh=fine,
        in_specs=(
            P(SEQ, TP),
            P(TP, None),
            P(SEQ, TP),
            P(),
            P(None, TP),
            P(SEQ, TP),
            P(),
            P(),
            P(),
            P(),
            P(SEQ, None, TP),
            P(SEQ, None, TP),
            P(TP, SEQ),
            P(TP, SEQ),
            P(SEQ),
            P(SEQ, TP),
            P(SEQ, TP),
        ),
        out_specs=(P(SEQ, TP), P(SEQ, TP)),
        check_vma=False,
    )
```

```python
import functools
import math

import jax
import jax.numpy as jnp
from jax import lax
from jax.experimental import pallas as pl
from jax.experimental.pallas import tpu as pltpu
from jax.sharding import Mesh, PartitionSpec as P

EPS = 1e-06
HD = 128
AXES = ("yh", "z", "c", "x", "yl")
SEQ = ("yh", "z", "c")
TP = ("x", "yl")
BF = jnp.bfloat16
F32 = jnp.float32


def shift(value, axis, step):
    size = lax.axis_size(axis)
    return lax.ppermute(value, axis, [(k, (k + step) % size) for k in range(size)])


def near(value, axis):
    return shift(value, axis, 1), shift(value, axis, -1)


def spread(value, axes):
    count = lax.axis_size(axes)
    copies = jnp.broadcast_to(value[None], (count,) + value.shape)
    return lax.all_to_all(copies, axes, split_axis=0, concat_axis=0, tiled=True)


def table(places):
    return jnp.stack([jnp.asarray(p, jnp.int32) for p in places])


def params(mib=48):
    return pltpu.CompilerParams(vmem_limit_bytes=mib * 1024 * 1024)


ANY = pl.BlockSpec(memory_space=pl.ANY)
VMEM = pl.BlockSpec(memory_space=pltpu.VMEM)
SMEM = pl.BlockSpec(memory_space=pltpu.SMEM)


def text_kernel(state_ref, gain_ref, proj_ref, out_ref):
    parts, rows, share = state_ref.shape
    square = jnp.zeros((rows, 1), F32)
    for t in range(parts):
        block = state_ref[t].astype(F32)
        square += jnp.sum(block * block, axis=-1, keepdims=True)
    factor = lax.rsqrt(square / (parts * share) + EPS)
    total = jnp.zeros(out_ref.shape, F32)
    for t in range(parts):
        normed = (state_ref[t].astype(F32) * factor * gain_ref[t]).astype(BF)
        total += jnp.dot(normed, proj_ref[t], preferred_element_type=F32)
    out_ref[...] = total.astype(BF)


def text_projection(state, gain, proj):
    parts, rows, share = state.shape
    return pl.pallas_call(
        text_kernel,
        out_shape=jax.ShapeDtypeStruct((rows, proj.shape[1]), BF),
        in_specs=[VMEM] * 3,
        out_specs=VMEM,
        compiler_params=params(),
        name="text_projection",
    )(state, gain.reshape(parts, 1, share), proj.reshape(parts, share, proj.shape[1]))


def qkv_kernel(a_index, count, place_ref, mod_ref, cos_ref, sin_ref, gain_ref, text_ref, *refs):
    arrays = a_index[-1][0] + 1
    a_arrays, w_pieces, refs = refs[:arrays], refs[arrays : arrays + count], refs[arrays + count :]
    q_ref, kv_ref, states, modded, weight, sems = refs
    parts, rows, share = states.shape
    width = parts * share
    depth = width // 16
    image_rows = rows // 5 * 4
    a_copies, w_copies = [], ([], [])
    for i, (array, index) in enumerate(a_index):
        dst = states.at[place_ref[i], pl.ds(0, image_rows)]
        a_copies.append(pltpu.make_async_copy(a_arrays[array].at[index], dst, sems.at[i]))
    dst = states.at[:, pl.ds(image_rows, rows - image_rows)]
    a_copies.append(pltpu.make_async_copy(text_ref, dst, sems.at[8]))
    for stream in range(2):
        for i, piece in enumerate(w_pieces):
            start = pl.multiple_of(place_ref[8 + i] * depth, depth)
            src = piece.at[pl.ds(3 * stream, 3)]
            dst = weight.at[pl.ds(3 * stream, 3), pl.ds(start, depth), :]
            sem = sems.at[9 + count * stream + i]
            w_copies[stream].append(pltpu.make_async_copy(src, dst, sem))
    for copy in a_copies + w_copies[0] + w_copies[1]:
        copy.start()
    for copy in a_copies:
        copy.wait()

    tile = 64

    def modulate(first, last, stream):
        @pl.loop(first // tile, last // tile)
        def _(step):
            here = pl.ds(pl.multiple_of(step * tile, tile), tile)
            total = jnp.zeros((tile, share), F32)
            for t in range(parts):
                total += states[t, here, :].astype(F32)
            center = jnp.sum(total, axis=-1, keepdims=True) / width
            total = jnp.zeros((tile, share), F32)
            for t in range(parts):
                shifted = states[t, here, :].astype(F32) - center
                total += shifted * shifted
            factor = lax.rsqrt(jnp.sum(total, axis=-1, keepdims=True) / width + EPS)
            for t in range(parts):
                cols = slice(t * share, (t + 1) * share)
                shifted = states[t, here, :].astype(F32) - center
                gain = 1.0 + mod_ref[stream, 1:2, cols]
                normed = shifted * factor * gain + mod_ref[stream, 0:1, cols]
                modded[here, cols] = normed.astype(BF)

    def prepare(flat, gain, cosine, sine):
        outs = []
        for h in range(share // HD):
            head = flat[:, h * HD : (h + 1) * HD]
            meansq = jnp.mean(head * head, axis=-1, keepdims=True)
            normed = head * lax.rsqrt(meansq + EPS) * gain
            outs.append(normed * cosine + pltpu.roll(normed, HD // 2, 1) * sine)
        return jnp.concatenate(outs, axis=1)

    def project(here, stream):
        def product(j):
            return jnp.dot(modded[here, :], weight[3 * stream + j], preferred_element_type=F32)

        cosine, sine = cos_ref[here, :], sin_ref[here, :]
        q = prepare(product(0), gain_ref[0:1, :], cosine, sine)
        q_ref[here, :] = (q * (math.log2(math.e) / math.sqrt(HD))).astype(BF)
        kv_ref[0, here, :] = prepare(product(1), gain_ref[1:2, :], cosine, sine).astype(BF)
        kv_ref[1, here, :] = product(2).astype(BF)

    modulate(0, image_rows, 0)
    modulate(image_rows, rows, 1)
    for copy in w_copies[0]:
        copy.wait()
    chunk = image_rows // 2

    @pl.loop(0, 2)
    def _(step):
        project(pl.ds(pl.multiple_of(step * chunk, chunk), chunk), 0)

    for copy in w_copies[1]:
        copy.wait()
    project(pl.ds(image_rows, rows - image_rows), 1)


def qkv(a_arrays, a_index, a_places, text_a, w_pieces, w_places, mods, cosine, sine, gains):
    parts, text_rows, share = text_a.shape
    rows = a_arrays[0].shape[-2] + text_rows
    width = parts * share
    arrays, count = len(a_arrays), len(w_pieces)
    return pl.pallas_call(
        functools.partial(qkv_kernel, a_index, count),
        out_shape=(
            jax.ShapeDtypeStruct((rows, share), BF),
            jax.ShapeDtypeStruct((2, rows, share), BF),
        ),
        in_specs=[SMEM, VMEM, VMEM, VMEM, VMEM] + [ANY] * (1 + arrays + count),
        out_specs=(VMEM, VMEM),
        scratch_shapes=[
            pltpu.VMEM((parts, rows, share), BF),
            pltpu.VMEM((rows, width), BF),
            pltpu.VMEM((6, width, share), BF),
            pltpu.SemaphoreType.DMA((9 + 2 * count,)),
        ],
        compiler_params=params(),
        name="qkv",
    )(table(a_places + w_places), mods, cosine, sine, gains, text_a, *a_arrays, *w_pieces)


def attention_kernel(nq, k_sizes, first, *refs):
    nk = len(k_sizes)
    q_refs, refs = refs[:nq], refs[nq:]
    k_refs, v_refs, refs = refs[:nk], refs[nk : 2 * nk], refs[2 * nk :]
    before, refs = ([], refs) if first else (refs[: 2 * nq], refs[2 * nq :])
    out_refs, tot_refs = refs[:nq], refs[nq : 2 * nq]
    keys, values = refs[2 * nq :]
    head = pl.program_id(0)
    at = 0
    for k_ref, v_ref, size in zip(k_refs, v_refs, k_sizes):
        keys[at : at + size, :] = k_ref[0]
        values[at : at + size, 0:HD] = v_ref[0]
        at += size

    @pl.when(head == 0)
    def _():
        values[:, HD:] = jnp.ones((values.shape[0], HD), BF)
        for i in range(nq):
            tot_refs[i][...] = jnp.zeros(tot_refs[i].shape, F32) if first else before[nq + i][...]

    rows = q_refs[0].shape[0]
    lane = lax.broadcasted_iota(jnp.int32, (rows, HD), 1)
    block = 256
    for i in range(nq):
        q = q_refs[i][...]
        total = jnp.zeros((rows, 2 * HD), F32)
        for start in range(0, keys.shape[0], block):
            stop = min(start + block, keys.shape[0])
            scores = lax.dot_general(
                q, keys[start:stop, :], (((1,), (1,)), ((), ())), preferred_element_type=F32
            )
            probs = jnp.exp2(scores).astype(BF)
            total += jnp.dot(probs, values[start:stop, :], preferred_element_type=F32)
        num = total[:, :HD]
        out_refs[i][...] = num if first else before[i][...] + num
        tot_refs[i][...] += jnp.where(lane == head, total[:, HD:], 0.0)


def attention(queries, kvs, before=()):
    rows, width = queries[0].shape
    keys = [(kv[0].reshape(-1, rows, width), 0) for kv in kvs]
    values = [(kv[-1].reshape(-1, rows, width), 2 - len(kv)) for kv in kvs]
    k_sizes = (rows,) * len(kvs)
    nq = len(queries)
    by_head = pl.BlockSpec((rows, HD), lambda h: (0, h))
    fixed = pl.BlockSpec((rows, HD), lambda h: (0, 0))
    sums = [by_head] * nq + [fixed] * nq
    inputs = nq + 2 * len(kvs)
    work = nq * rows * len(kvs) * rows * width
    return pl.pallas_call(
        functools.partial(attention_kernel, nq, k_sizes, not before),
        grid=(width // HD,),
        out_shape=[jax.ShapeDtypeStruct((rows, width), F32)] * nq
        + [jax.ShapeDtypeStruct((rows, HD), F32)] * nq,
        in_specs=[by_head] * nq
        + [
            pl.BlockSpec((1, rows, HD), functools.partial(lambda i, h: (i, 0, h), i))
            for _, i in keys + values
        ]
        + (sums if before else []),
        out_specs=sums,
        input_output_aliases={inputs + i: i for i in range(2 * nq)} if before else {},
        scratch_shapes=[
            pltpu.VMEM((sum(k_sizes), HD), BF),
            pltpu.VMEM((sum(k_sizes), 2 * HD), BF),
        ],
        compiler_params=params(),
        cost_estimate=pl.CostEstimate(
            flops=8 * work, bytes_accessed=8 * nq * rows * width, transcendentals=work // HD
        ),
        name="attention",
    )(*queries, *[k for k, _ in keys + values], *before)


def combine_kernel(num_ref, other_ref, back_ref, tot_ref, other_tot_ref, out_ref):
    share = num_ref.shape[1]
    for h in range(share // HD):
        cols = slice(h * HD, (h + 1) * HD)
        lane, low = slice(share + h, share + h + 1), slice(share + 64 + h, share + 65 + h)
        num = num_ref[:, cols] + other_ref[:, cols] + back_ref[:, cols].astype(F32)
        tot = tot_ref[:, h : h + 1] + other_tot_ref[:, h : h + 1]
        tot += back_ref[:, lane].astype(F32) + back_ref[:, low].astype(F32)
        out_ref[:, cols] = (num / tot).astype(BF)


def combine(num, other, back, tot, other_tot):
    return pl.pallas_call(
        combine_kernel,
        out_shape=jax.ShapeDtypeStruct(num.shape, BF),
        in_specs=[VMEM] * 5,
        out_specs=VMEM,
        compiler_params=params(),
        name="combine",
    )(num, other, back, tot, other_tot)


def out_kernel(place_ref, own_ref, other_ref, weight_ref, out_ref, attended):
    rows, share = own_ref.shape
    image_rows = rows // 5 * 4

    @pl.when(pl.program_id(0) == 0)
    def _():
        first = place_ref[0] == 0
        attended[:, :share] = jnp.where(first, own_ref[...], other_ref[...])
        attended[:, share:] = jnp.where(first, other_ref[...], own_ref[...])

    for stream, here in ((0, slice(0, image_rows)), (1, slice(image_rows, rows))):
        halves = [weight_ref[2 * y : 2 * y + 2, stream].reshape(share, share) for y in range(2)]
        out_ref[0, here, :] = lax.dot_general(
            attended[here, :],
            jnp.concatenate(halves, axis=1),
            (((1,), (1,)), ((), ())),
            preferred_element_type=F32,
        ).astype(BF)


def out_projection(own, other, weight, yl):
    rows, share = own.shape
    whole = pl.BlockSpec((rows, share), lambda x: (0, 0))
    return pl.pallas_call(
        out_kernel,
        grid=(4,),
        out_shape=jax.ShapeDtypeStruct((4, rows, share), BF),
        in_specs=[SMEM, whole, whole]
        + [pl.BlockSpec((4,) + weight.shape[1:], lambda x: (x, 0, 0, 0))],
        out_specs=pl.BlockSpec((1, rows, share), lambda x: (x, 0, 0)),
        scratch_shapes=[pltpu.VMEM((rows, 2 * share), BF)],
        compiler_params=params(),
        name="out_projection",
    )(table([yl]), own, other, weight)


def angles_of(positions):
    freqs = 10000.0 ** (-(jnp.arange(HD // 2, dtype=F32) * 2.0) / HD)
    angles = positions[:, None] * freqs[None, :]
    cosine, sine = jnp.cos(angles), jnp.sin(angles)
    return jnp.concatenate([cosine, cosine], axis=1), jnp.concatenate([-sine, sine], axis=1)


def shards(
    cond_hidden,
    cond_down,
    cond_resid,
    cond_gain,
    text_proj,
    image_states,
    image_mod,
    text_mod,
    query_gain,
    key_gain,
    image_qkv,
    text_qkv,
    image_out,
    text_out,
    cond_pos,
    image_cache,
    text_cache,
):
    seq_index = lax.axis_index(SEQ)
    tp_index = lax.axis_index(TP)
    image_rows, share = image_states.shape
    text_rows = cond_hidden.shape[0]

    yh, z, c, x, yl = (lax.axis_index(a) for a in AXES)
    together = lax.optimization_barrier
    outs = jnp.stack([jnp.transpose(image_out), jnp.transpose(text_out)])
    weight = jnp.transpose(jnp.concatenate([image_qkv, text_qkv], axis=1), (1, 0, 2))

    a_pair = shift(image_states, "yl", 1)
    a_near = near(image_states, "x")
    w_pair = shift(weight, "yh", 1)
    cond_hidden, a_pair, a_near = together((cond_hidden, a_pair, a_near))

    w_near = near(weight, "z")
    a_next = near(a_pair, "x")
    partial_value = jnp.dot(cond_hidden, cond_down, preferred_element_type=F32).astype(BF)
    enc_share = cond_down.shape[1] // 8
    sent = jnp.transpose(partial_value.reshape(text_rows, 8, enc_share), (1, 0, 2))
    got = lax.all_to_all(sent, TP, split_axis=0, concat_axis=0, tiled=True)
    got, a_near, a_next, w_near, w_pair, outs = together(
        (got, a_near, a_next, w_near, w_pair, outs)
    )

    a_far = (shift(a_near[0], "x", 1), shift(a_next[1], "x", -1))
    w_next = near(w_pair, "z")
    turned = [
        (4 * zh + 2 * zl + y, 4 * zh + 2 * y + zl)
        for zh in range(2)
        for zl in range(2)
        for y in range(2)
    ]
    outs = lax.ppermute(outs, ("z", "yl"), turned)
    cond_state = (jnp.sum(got.astype(F32), axis=0) + cond_resid.astype(F32)).astype(BF)
    state = spread(cond_state, TP)
    state, a_far, w_near, w_next, outs = together((state, a_far, w_near, w_next, outs))
    out_w = lax.all_gather(outs, SEQ)

    text_states = text_projection(state, cond_gain, text_proj)
    text_a = spread(text_states, TP)
    w_far = (shift(w_near[0], "z", 1), shift(w_next[1], "z", -1))
    text_a, w_far = together((text_a, w_far))

    blocks = [(p, d) for p in range(2) for d in (0, 3, 1, 2)]
    a_arrays = [image_states, *a_near, a_far[0], a_pair, *a_next, a_far[1]]
    a_index = tuple((i, ()) for i in range(8))
    a_places = [(x + d) % 4 * 2 + (yl + p) % 2 for p, d in blocks]
    w_arrays = [weight, *w_near, w_far[0], w_pair, *w_next, w_far[1]]
    w_arrays += [shift(w, "c", 1) for w in w_arrays]

    gains = jnp.stack([query_gain, key_gain])
    image_pos = (seq_index * image_rows + jnp.arange(image_rows)).astype(F32)
    w_places = [
        (yh + p) % 2 * 8 + (z + d) % 4 * 2 + (c + k) % 2 for k in range(2) for p, d in blocks
    ]
    query, kv = qkv(
        a_arrays,
        a_index,
        a_places,
        text_a,
        w_arrays,
        w_places,
        jnp.stack([image_mod, text_mod]),
        *angles_of(jnp.concatenate([image_pos, cond_pos.astype(F32)])),
        gains,
    )
    pair_query = shift(query, "yh", 1)
    kv_left, kv_right = near(kv, "z")
    core_query = shift(query, "c", 1)
    own_queries = [query, core_query]
    own = attention(own_queries, [(kv,)])
    pair_query, own = together((pair_query, own))
    pair_queries = [pair_query, shift(pair_query, "c", 1)]
    pair = attention(pair_queries, [(kv,)])
    pair, kv_left, kv_right = together((pair, kv_left, kv_right))
    kv_far = (shift(kv_left[0], "z", 1), shift(kv_right[1], "z", -1))
    pair = attention(pair_queries, [(kv_left,), (kv_right,)], pair)
    pair, kv_far = together((pair, kv_far))
    pair = attention(pair_queries, [kv_far], pair)

    sent_num = pair[0] + shift(pair[1], "c", 1)
    sent_tot = pair[2] + shift(pair[3], "c", 1)
    high = sent_tot.astype(BF)
    low = (sent_tot - high.astype(F32)).astype(BF)
    mixed = jnp.concatenate([sent_num.astype(BF), high[:, :64], low[:, :64]], axis=1)
    mixed, own = together((mixed, own))
    back = shift(mixed, "yh", 1)
    own = attention(own_queries, [(kv_left,), (kv_right,), kv_far], own)
    back, own = together((back, own))
    attended = combine(own[0], shift(own[1], "c", 1), back, own[2], shift(own[3], "c", 1))

    parts = out_projection(attended, shift(attended, "yl", 1), out_w, yl)
    got = lax.all_to_all(parts, "x", split_axis=0, concat_axis=0, tiled=True)
    branch = jnp.sum(got.astype(F32), axis=0)

    def finish(states, mod, rows, cache):
        gates = lax.dynamic_slice_in_dim(mod, tp_index * share, share, 1)
        return (
            states.astype(F32) + gates[2] * branch[rows] + gates[3] * cache.astype(F32)
        ).astype(BF)

    return (
        finish(image_states, image_mod, slice(0, image_rows), image_cache),
        finish(text_states, text_mod, slice(image_rows, None), text_cache),
    )


def solution(mesh):
    fine = Mesh(mesh.devices.reshape(2, 4, 2, 4, 2), AXES)
    return jax.shard_map(
        shards,
        mesh=fine,
        in_specs=(
            P(SEQ, TP),
            P(TP, None),
            P(SEQ, TP),
            P(),
            P(None, TP),
            P(SEQ, TP),
            P(),
            P(),
            P(),
            P(),
            P(SEQ, None, TP),
            P(SEQ, None, TP),
            P(TP, SEQ),
            P(TP, SEQ),
            P(SEQ),
            P(SEQ, TP),
            P(SEQ, TP),
        ),
        out_specs=(P(SEQ, TP), P(SEQ, TP)),
        check_vma=False,
    )
```

```python
import functools
import math

import jax
import jax.numpy as jnp
from jax import lax
from jax.experimental import pallas as pl
from jax.experimental.pallas import tpu as pltpu
from jax.sharding import Mesh, PartitionSpec as P

EPS = 1e-06
HD = 128
AXES = ("yh", "z", "c", "x", "yl")
SEQ = ("yh", "z", "c")
TP = ("x", "yl")
BF = jnp.bfloat16
F32 = jnp.float32


def shift(value, axis, step):
    size = lax.axis_size(axis)
    return lax.ppermute(value, axis, [(k, (k + step) % size) for k in range(size)])


def near(value, axis):
    return shift(value, axis, 1), shift(value, axis, -1)


def spread(value, axes):
    count = lax.axis_size(axes)
    copies = jnp.broadcast_to(value[None], (count,) + value.shape)
    return lax.all_to_all(copies, axes, split_axis=0, concat_axis=0, tiled=True)


def table(places):
    return jnp.stack([jnp.asarray(p, jnp.int32) for p in places])


def params(mib=48):
    return pltpu.CompilerParams(vmem_limit_bytes=mib * 1024 * 1024)


ANY = pl.BlockSpec(memory_space=pl.ANY)
VMEM = pl.BlockSpec(memory_space=pltpu.VMEM)
SMEM = pl.BlockSpec(memory_space=pltpu.SMEM)


def text_kernel(state_ref, gain_ref, proj_ref, out_ref):
    parts, rows, share = state_ref.shape
    square = jnp.zeros((rows, 1), F32)
    for t in range(parts):
        block = state_ref[t].astype(F32)
        square += jnp.sum(block * block, axis=-1, keepdims=True)
    factor = lax.rsqrt(square / (parts * share) + EPS)
    total = jnp.zeros(out_ref.shape, F32)
    for t in range(parts):
        normed = (state_ref[t].astype(F32) * factor * gain_ref[t]).astype(BF)
        total += jnp.dot(normed, proj_ref[t], preferred_element_type=F32)
    out_ref[...] = total.astype(BF)


def text_projection(state, gain, proj):
    parts, rows, share = state.shape
    return pl.pallas_call(
        text_kernel,
        out_shape=jax.ShapeDtypeStruct((rows, proj.shape[1]), BF),
        in_specs=[VMEM] * 3,
        out_specs=VMEM,
        compiler_params=params(),
        name="text_projection",
    )(state, gain.reshape(parts, 1, share), proj.reshape(parts, share, proj.shape[1]))


def normalise(states, mod_ref, out_ref, first):
    parts, rows, share = states.shape
    width = parts * share
    tile = 64

    @pl.loop(0, rows // tile)
    def _(step):
        here = pl.ds(pl.multiple_of(step * tile, tile), tile)
        there = pl.ds(pl.multiple_of(first + step * tile, tile), tile)
        total = jnp.zeros((tile, share), F32)
        for t in range(parts):
            total += states[t, here, :].astype(F32)
        center = jnp.sum(total, axis=-1, keepdims=True) / width
        total = jnp.zeros((tile, share), F32)
        for t in range(parts):
            shifted = states[t, here, :].astype(F32) - center
            total += shifted * shifted
        factor = lax.rsqrt(jnp.sum(total, axis=-1, keepdims=True) / width + EPS)
        for t in range(parts):
            cols = slice(t * share, (t + 1) * share)
            shifted = states[t, here, :].astype(F32) - center
            normed = shifted * factor * (1.0 + mod_ref[1:2, cols]) + mod_ref[0:1, cols]
            out_ref[there, cols] = normed.astype(BF)


def modulate_kernel(count, place_ref, mod_ref, *refs):
    pieces, (out_ref, states, sems) = refs[:count], refs[count:]
    copies = [
        pltpu.make_async_copy(piece, states.at[place_ref[i]], sems.at[i])
        for i, piece in enumerate(pieces)
    ]
    for copy in copies:
        copy.start()
    for copy in copies:
        copy.wait()
    normalise(states, mod_ref, out_ref, 0)


def modulate(pieces, places, mod):
    rows, share = pieces[0].shape
    count = len(pieces)
    return pl.pallas_call(
        functools.partial(modulate_kernel, count),
        out_shape=jax.ShapeDtypeStruct((rows, count * share), BF),
        in_specs=[SMEM, VMEM] + [ANY] * count,
        out_specs=VMEM,
        scratch_shapes=[
            pltpu.VMEM((count, rows, share), BF),
            pltpu.SemaphoreType.DMA((count,)),
        ],
        compiler_params=params(),
        name="modulate",
    )(table(places), mod, *pieces)


def qkv_kernel(count, place_ref, mod_ref, cos_ref, sin_ref, gain_ref, image_ref, *refs):
    text_ref, w_pieces, refs = refs[0], refs[1 : 1 + count], refs[1 + count :]
    q_ref, kv_ref, states, modded, weight, sems = refs
    share = states.shape[2]
    rows, width = modded.shape
    depth = width // 16
    image_rows = image_ref.shape[0]
    image_copy = pltpu.make_async_copy(
        image_ref, modded.at[pl.ds(0, image_rows)], sems.at[2 * count]
    )
    text_copy = pltpu.make_async_copy(text_ref, states, sems.at[2 * count + 1])
    w_copies = ([], [])
    for stream in range(2):
        for i, piece in enumerate(w_pieces):
            start = pl.multiple_of(place_ref[i] * depth, depth)
            src = piece.at[pl.ds(3 * stream, 3)]
            dst = weight.at[pl.ds(3 * stream, 3), pl.ds(start, depth), :]
            sem = sems.at[count * stream + i]
            w_copies[stream].append(pltpu.make_async_copy(src, dst, sem))
    for copy in [text_copy, image_copy] + w_copies[0] + w_copies[1]:
        copy.start()
    text_copy.wait()
    normalise(states, mod_ref, modded, image_rows)

    def prepare(flat, gain, cosine, sine):
        outs = []
        for h in range(share // HD):
            head = flat[:, h * HD : (h + 1) * HD]
            meansq = jnp.mean(head * head, axis=-1, keepdims=True)
            normed = head * lax.rsqrt(meansq + EPS) * gain
            outs.append(normed * cosine + pltpu.roll(normed, HD // 2, 1) * sine)
        return jnp.concatenate(outs, axis=1)

    def project(here, stream):
        def product(j):
            return jnp.dot(modded[here, :], weight[3 * stream + j], preferred_element_type=F32)

        cosine, sine = cos_ref[here, :], sin_ref[here, :]
        q = prepare(product(0), gain_ref[0:1, :], cosine, sine)
        q_ref[here, :] = (q * (math.log2(math.e) / math.sqrt(HD))).astype(BF)
        kv_ref[0, here, :] = prepare(product(1), gain_ref[1:2, :], cosine, sine).astype(BF)
        kv_ref[1, here, :] = product(2).astype(BF)

    image_copy.wait()
    for copy in w_copies[0]:
        copy.wait()
    chunk = image_rows // 2

    @pl.loop(0, 2)
    def _(step):
        project(pl.ds(pl.multiple_of(step * chunk, chunk), chunk), 0)

    for copy in w_copies[1]:
        copy.wait()
    project(pl.ds(image_rows, rows - image_rows), 1)


def qkv(image, text_a, w_pieces, w_places, mod, cosine, sine, gains):
    parts, text_rows, share = text_a.shape
    image_rows, width = image.shape
    rows = image_rows + text_rows
    count = len(w_pieces)
    return pl.pallas_call(
        functools.partial(qkv_kernel, count),
        out_shape=(
            jax.ShapeDtypeStruct((rows, share), BF),
            jax.ShapeDtypeStruct((2, rows, share), BF),
        ),
        in_specs=[SMEM, VMEM, VMEM, VMEM, VMEM] + [ANY] * (2 + count),
        out_specs=(VMEM, VMEM),
        scratch_shapes=[
            pltpu.VMEM((parts, text_rows, share), BF),
            pltpu.VMEM((rows, width), BF),
            pltpu.VMEM((6, width, share), BF),
            pltpu.SemaphoreType.DMA((2 * count + 2,)),
        ],
        compiler_params=params(),
        name="qkv",
    )(table(w_places), mod, cosine, sine, gains, image, text_a, *w_pieces)


def attention_kernel(nq, k_sizes, first, *refs):
    nk = len(k_sizes)
    q_refs, refs = refs[:nq], refs[nq:]
    k_refs, v_refs, refs = refs[:nk], refs[nk : 2 * nk], refs[2 * nk :]
    before, refs = ([], refs) if first else (refs[: 2 * nq], refs[2 * nq :])
    out_refs, tot_refs = refs[:nq], refs[nq : 2 * nq]
    keys, values = refs[2 * nq :]
    head = pl.program_id(0)
    at = 0
    for k_ref, v_ref, size in zip(k_refs, v_refs, k_sizes):
        keys[at : at + size, :] = k_ref[0]
        values[at : at + size, 0:HD] = v_ref[0]
        at += size

    @pl.when(head == 0)
    def _():
        values[:, HD:] = jnp.ones((values.shape[0], HD), BF)
        for i in range(nq):
            tot_refs[i][...] = jnp.zeros(tot_refs[i].shape, F32) if first else before[nq + i][...]

    rows = q_refs[0].shape[0]
    lane = lax.broadcasted_iota(jnp.int32, (rows, HD), 1)
    block = 256
    for i in range(nq):
        q = q_refs[i][...]
        total = jnp.zeros((rows, 2 * HD), F32)
        for start in range(0, keys.shape[0], block):
            stop = min(start + block, keys.shape[0])
            scores = lax.dot_general(
                q, keys[start:stop, :], (((1,), (1,)), ((), ())), preferred_element_type=F32
            )
            probs = jnp.exp2(scores).astype(BF)
            total += jnp.dot(probs, values[start:stop, :], preferred_element_type=F32)
        num = total[:, :HD]
        out_refs[i][...] = num if first else before[i][...] + num
        tot_refs[i][...] += jnp.where(lane == head, total[:, HD:], 0.0)


def attention(queries, kvs, before=()):
    rows, width = queries[0].shape
    keys = [(kv[0].reshape(-1, rows, width), 0) for kv in kvs]
    values = [(kv[-1].reshape(-1, rows, width), 2 - len(kv)) for kv in kvs]
    k_sizes = (rows,) * len(kvs)
    nq = len(queries)
    by_head = pl.BlockSpec((rows, HD), lambda h: (0, h))
    fixed = pl.BlockSpec((rows, HD), lambda h: (0, 0))
    sums = [by_head] * nq + [fixed] * nq
    inputs = nq + 2 * len(kvs)
    work = nq * rows * len(kvs) * rows * width
    return pl.pallas_call(
        functools.partial(attention_kernel, nq, k_sizes, not before),
        grid=(width // HD,),
        out_shape=[jax.ShapeDtypeStruct((rows, width), F32)] * nq
        + [jax.ShapeDtypeStruct((rows, HD), F32)] * nq,
        in_specs=[by_head] * nq
        + [
            pl.BlockSpec((1, rows, HD), functools.partial(lambda i, h: (i, 0, h), i))
            for _, i in keys + values
        ]
        + (sums if before else []),
        out_specs=sums,
        input_output_aliases={inputs + i: i for i in range(2 * nq)} if before else {},
        scratch_shapes=[
            pltpu.VMEM((sum(k_sizes), HD), BF),
            pltpu.VMEM((sum(k_sizes), 2 * HD), BF),
        ],
        compiler_params=params(),
        cost_estimate=pl.CostEstimate(
            flops=8 * work, bytes_accessed=8 * nq * rows * width, transcendentals=work // HD
        ),
        name="attention",
    )(*queries, *[k for k, _ in keys + values], *before)


def combine_kernel(num_ref, other_ref, back_ref, tot_ref, other_tot_ref, out_ref):
    share = num_ref.shape[1]
    for h in range(share // HD):
        cols = slice(h * HD, (h + 1) * HD)
        lane, low = slice(share + h, share + h + 1), slice(share + 64 + h, share + 65 + h)
        num = num_ref[:, cols] + other_ref[:, cols] + back_ref[:, cols].astype(F32)
        tot = tot_ref[:, h : h + 1] + other_tot_ref[:, h : h + 1]
        tot += back_ref[:, lane].astype(F32) + back_ref[:, low].astype(F32)
        out_ref[:, cols] = (num / tot).astype(BF)


def combine(num, other, back, tot, other_tot):
    return pl.pallas_call(
        combine_kernel,
        out_shape=jax.ShapeDtypeStruct(num.shape, BF),
        in_specs=[VMEM] * 5,
        out_specs=VMEM,
        compiler_params=params(),
        name="combine",
    )(num, other, back, tot, other_tot)


def out_kernel(place_ref, own_ref, other_ref, weight_ref, out_ref, attended):
    rows, share = own_ref.shape
    image_rows = rows // 5 * 4

    @pl.when(pl.program_id(0) == 0)
    def _():
        first = place_ref[0] == 0
        attended[:, :share] = jnp.where(first, own_ref[...], other_ref[...])
        attended[:, share:] = jnp.where(first, other_ref[...], own_ref[...])

    for stream, here in ((0, slice(0, image_rows)), (1, slice(image_rows, rows))):
        halves = [weight_ref[2 * y : 2 * y + 2, stream].reshape(share, share) for y in range(2)]
        out_ref[0, here, :] = lax.dot_general(
            attended[here, :],
            jnp.concatenate(halves, axis=1),
            (((1,), (1,)), ((), ())),
            preferred_element_type=F32,
        ).astype(BF)


def out_projection(own, other, weight, yl):
    rows, share = own.shape
    whole = pl.BlockSpec((rows, share), lambda x: (0, 0))
    return pl.pallas_call(
        out_kernel,
        grid=(4,),
        out_shape=jax.ShapeDtypeStruct((4, rows, share), BF),
        in_specs=[SMEM, whole, whole]
        + [pl.BlockSpec((4,) + weight.shape[1:], lambda x: (x, 0, 0, 0))],
        out_specs=pl.BlockSpec((1, rows, share), lambda x: (x, 0, 0)),
        scratch_shapes=[pltpu.VMEM((rows, 2 * share), BF)],
        compiler_params=params(),
        name="out_projection",
    )(table([yl]), own, other, weight)


def angles_of(positions):
    freqs = 10000.0 ** (-(jnp.arange(HD // 2, dtype=F32) * 2.0) / HD)
    angles = positions[:, None] * freqs[None, :]
    cosine, sine = jnp.cos(angles), jnp.sin(angles)
    return jnp.concatenate([cosine, cosine], axis=1), jnp.concatenate([-sine, sine], axis=1)


def shards(
    cond_hidden,
    cond_down,
    cond_resid,
    cond_gain,
    text_proj,
    image_states,
    image_mod,
    text_mod,
    query_gain,
    key_gain,
    image_qkv,
    text_qkv,
    image_out,
    text_out,
    cond_pos,
    image_cache,
    text_cache,
):
    seq_index = lax.axis_index(SEQ)
    tp_index = lax.axis_index(TP)
    image_rows, share = image_states.shape
    text_rows = cond_hidden.shape[0]

    yh, z, c, x, yl = (lax.axis_index(a) for a in AXES)
    together = lax.optimization_barrier
    outs = jnp.stack([jnp.transpose(image_out), jnp.transpose(text_out)])
    weight = jnp.transpose(jnp.concatenate([image_qkv, text_qkv], axis=1), (1, 0, 2))

    turned = [
        (4 * zh + 2 * zl + y, 4 * zh + 2 * y + zl)
        for zh in range(2)
        for zl in range(2)
        for y in range(2)
    ]
    outs = lax.ppermute(outs, ("z", "yl"), turned)
    a_pair = shift(image_states, "yl", 1)
    a_near = near(image_states, "x")
    w_pair = shift(weight, "yh", 1)
    cond_hidden, a_pair, a_near, outs = together((cond_hidden, a_pair, a_near, outs))

    w_near = near(weight, "z")
    a_next = near(a_pair, "x")
    partial_value = jnp.dot(cond_hidden, cond_down, preferred_element_type=F32).astype(BF)
    enc_share = cond_down.shape[1] // 8
    sent = jnp.transpose(partial_value.reshape(text_rows, 8, enc_share), (1, 0, 2))
    got = lax.all_to_all(sent, TP, split_axis=0, concat_axis=0, tiled=True)
    got, a_near, a_next, w_near, w_pair, outs = together(
        (got, a_near, a_next, w_near, w_pair, outs)
    )

    out_w = lax.all_gather(outs, SEQ)
    a_far = (shift(a_near[0], "x", 1), shift(a_next[1], "x", -1))
    w_next = near(w_pair, "z")
    cond_state = (jnp.sum(got.astype(F32), axis=0) + cond_resid.astype(F32)).astype(BF)
    state = spread(cond_state, TP)
    state, a_far, w_near, w_next = together((state, a_far, w_near, w_next))

    text_states = text_projection(state, cond_gain, text_proj)
    text_a = spread(text_states, TP)
    w_far = (shift(w_near[0], "z", 1), shift(w_next[1], "z", -1))

    blocks = [(p, d) for p in range(2) for d in (0, 3, 1, 2)]
    a_arrays = [image_states, *a_near, a_far[0], a_pair, *a_next, a_far[1]]
    a_places = [(x + d) % 4 * 2 + (yl + p) % 2 for p, d in blocks]
    image_modded = modulate(a_arrays, a_places, image_mod)
    text_a, w_far, image_modded = together((text_a, w_far, image_modded))

    w_arrays = [weight, *w_near, w_far[0], w_pair, *w_next, w_far[1]]
    w_arrays += [shift(w, "c", 1) for w in w_arrays]

    gains = jnp.stack([query_gain, key_gain])
    image_pos = (seq_index * image_rows + jnp.arange(image_rows)).astype(F32)
    w_places = [
        (yh + p) % 2 * 8 + (z + d) % 4 * 2 + (c + k) % 2 for k in range(2) for p, d in blocks
    ]
    query, kv = qkv(
        image_modded,
        text_a,
        w_arrays,
        w_places,
        text_mod,
        *angles_of(jnp.concatenate([image_pos, cond_pos.astype(F32)])),
        gains,
    )
    pair_query = shift(query, "yh", 1)
    kv_left, kv_right = near(kv, "z")
    core_query = shift(query, "c", 1)
    own_queries = [query, core_query]
    own = attention(own_queries, [(kv,)])
    pair_query, own = together((pair_query, own))
    pair_queries = [pair_query, shift(pair_query, "c", 1)]
    pair = attention(pair_queries, [(kv,)])
    pair, kv_left, kv_right = together((pair, kv_left, kv_right))
    kv_far = (shift(kv_left[0], "z", 1), shift(kv_right[1], "z", -1))
    pair = attention(pair_queries, [(kv_left,), (kv_right,)], pair)
    pair, kv_far = together((pair, kv_far))
    pair = attention(pair_queries, [kv_far], pair)

    sent_num = pair[0] + shift(pair[1], "c", 1)
    sent_tot = pair[2] + shift(pair[3], "c", 1)
    high = sent_tot.astype(BF)
    low = (sent_tot - high.astype(F32)).astype(BF)
    mixed = jnp.concatenate([sent_num.astype(BF), high[:, :64], low[:, :64]], axis=1)
    mixed, own = together((mixed, own))
    back = shift(mixed, "yh", 1)
    own = attention(own_queries, [(kv_left,), (kv_right,), kv_far], own)
    back, own = together((back, own))
    attended = combine(own[0], shift(own[1], "c", 1), back, own[2], shift(own[3], "c", 1))

    parts = out_projection(attended, shift(attended, "yl", 1), out_w, yl)
    got = lax.all_to_all(parts, "x", split_axis=0, concat_axis=0, tiled=True)
    branch = jnp.sum(got.astype(F32), axis=0)

    def finish(states, mod, rows, cache):
        gates = lax.dynamic_slice_in_dim(mod, tp_index * share, share, 1)
        return (
            states.astype(F32) + gates[2] * branch[rows] + gates[3] * cache.astype(F32)
        ).astype(BF)

    return (
        finish(image_states, image_mod, slice(0, image_rows), image_cache),
        finish(text_states, text_mod, slice(image_rows, None), text_cache),
    )


def solution(mesh):
    fine = Mesh(mesh.devices.reshape(2, 4, 2, 4, 2), AXES)
    return jax.shard_map(
        shards,
        mesh=fine,
        in_specs=(
            P(SEQ, TP),
            P(TP, None),
            P(SEQ, TP),
            P(),
            P(None, TP),
            P(SEQ, TP),
            P(),
            P(),
            P(),
            P(),
            P(SEQ, None, TP),
            P(SEQ, None, TP),
            P(TP, SEQ),
            P(TP, SEQ),
            P(SEQ),
            P(SEQ, TP),
            P(SEQ, TP),
        ),
        out_specs=(P(SEQ, TP), P(SEQ, TP)),
        check_vma=False,
    )
```

```python
import functools
import math

import jax
import jax.numpy as jnp
from jax import lax
from jax.experimental import pallas as pl
from jax.experimental.pallas import tpu as pltpu
from jax.sharding import Mesh, PartitionSpec as P

EPS = 1e-06
HD = 128
AXES = ("yh", "z", "c", "x", "yl")
SEQ = ("yh", "z", "c")
TP = ("x", "yl")
BF = jnp.bfloat16
F32 = jnp.float32


def shift(value, axis, step):
    size = lax.axis_size(axis)
    return lax.ppermute(value, axis, [(k, (k + step) % size) for k in range(size)])


def near(value, axis):
    return shift(value, axis, 1), shift(value, axis, -1)


def spread(value, axes):
    count = lax.axis_size(axes)
    copies = jnp.broadcast_to(value[None], (count,) + value.shape)
    return lax.all_to_all(copies, axes, split_axis=0, concat_axis=0, tiled=True)


def table(places):
    return jnp.stack([jnp.asarray(p, jnp.int32) for p in places])


def params(mib=48):
    return pltpu.CompilerParams(vmem_limit_bytes=mib * 1024 * 1024)


ANY = pl.BlockSpec(memory_space=pl.ANY)
VMEM = pl.BlockSpec(memory_space=pltpu.VMEM)
SMEM = pl.BlockSpec(memory_space=pltpu.SMEM)


def text_kernel(state_ref, gain_ref, proj_ref, out_ref):
    parts, rows, share = state_ref.shape
    square = jnp.zeros((rows, 1), F32)
    for t in range(parts):
        block = state_ref[t].astype(F32)
        square += jnp.sum(block * block, axis=-1, keepdims=True)
    factor = lax.rsqrt(square / (parts * share) + EPS)
    total = jnp.zeros(out_ref.shape, F32)
    for t in range(parts):
        normed = (state_ref[t].astype(F32) * factor * gain_ref[t]).astype(BF)
        total += jnp.dot(normed, proj_ref[t], preferred_element_type=F32)
    out_ref[...] = total.astype(BF)


def text_projection(state, gain, proj):
    parts, rows, share = state.shape
    return pl.pallas_call(
        text_kernel,
        out_shape=jax.ShapeDtypeStruct((rows, proj.shape[1]), BF),
        in_specs=[VMEM] * 3,
        out_specs=VMEM,
        compiler_params=params(),
        name="text_projection",
    )(state, gain.reshape(parts, 1, share), proj.reshape(parts, share, proj.shape[1]))


def normalise(states, mod_ref, out_ref, first):
    parts, rows, share = states.shape
    width = parts * share
    tile = 64

    @pl.loop(0, rows // tile)
    def _(step):
        here = pl.ds(pl.multiple_of(step * tile, tile), tile)
        there = pl.ds(pl.multiple_of(first + step * tile, tile), tile)
        total = jnp.zeros((tile, share), F32)
        for t in range(parts):
            total += states[t, here, :].astype(F32)
        center = jnp.sum(total, axis=-1, keepdims=True) / width
        total = jnp.zeros((tile, share), F32)
        for t in range(parts):
            shifted = states[t, here, :].astype(F32) - center
            total += shifted * shifted
        factor = lax.rsqrt(jnp.sum(total, axis=-1, keepdims=True) / width + EPS)
        for t in range(parts):
            cols = slice(t * share, (t + 1) * share)
            shifted = states[t, here, :].astype(F32) - center
            normed = shifted * factor * (1.0 + mod_ref[1:2, cols]) + mod_ref[0:1, cols]
            out_ref[there, cols] = normed.astype(BF)


def modulate_kernel(count, place_ref, mod_ref, *refs):
    pieces, (out_ref, states, sems) = refs[:count], refs[count:]
    copies = [
        pltpu.make_async_copy(piece, states.at[place_ref[i]], sems.at[i])
        for i, piece in enumerate(pieces)
    ]
    for copy in copies:
        copy.start()
    for copy in copies:
        copy.wait()
    normalise(states, mod_ref, out_ref, 0)


def modulate(pieces, places, mod):
    rows, share = pieces[0].shape
    count = len(pieces)
    return pl.pallas_call(
        functools.partial(modulate_kernel, count),
        out_shape=jax.ShapeDtypeStruct((rows, count * share), BF),
        in_specs=[SMEM, VMEM] + [ANY] * count,
        out_specs=VMEM,
        scratch_shapes=[
            pltpu.VMEM((count, rows, share), BF),
            pltpu.SemaphoreType.DMA((count,)),
        ],
        compiler_params=params(),
        name="modulate",
    )(table(places), mod, *pieces)


def qkv_kernel(count, place_ref, mod_ref, cos_ref, sin_ref, gain_ref, image_ref, *refs):
    text_ref, w_pieces, refs = refs[0], refs[1 : 1 + count], refs[1 + count :]
    q_ref, kv_ref, states, modded, weight, sems = refs
    share = states.shape[2]
    rows, width = modded.shape
    depth = width // 16
    image_rows = image_ref.shape[0]
    image_copy = pltpu.make_async_copy(
        image_ref, modded.at[pl.ds(0, image_rows)], sems.at[2 * count]
    )
    text_copy = pltpu.make_async_copy(text_ref, states, sems.at[2 * count + 1])
    w_copies = ([], [])
    for stream in range(2):
        for i, piece in enumerate(w_pieces):
            start = pl.multiple_of(place_ref[i] * depth, depth)
            src = piece.at[pl.ds(3 * stream, 3)]
            dst = weight.at[pl.ds(3 * stream, 3), pl.ds(start, depth), :]
            sem = sems.at[count * stream + i]
            w_copies[stream].append(pltpu.make_async_copy(src, dst, sem))
    for copy in [text_copy, image_copy] + w_copies[0] + w_copies[1]:
        copy.start()
    text_copy.wait()
    normalise(states, mod_ref, modded, image_rows)

    def prepare(flat, gain, cosine, sine):
        outs = []
        for h in range(share // HD):
            head = flat[:, h * HD : (h + 1) * HD]
            meansq = jnp.mean(head * head, axis=-1, keepdims=True)
            normed = head * lax.rsqrt(meansq + EPS) * gain
            outs.append(normed * cosine + pltpu.roll(normed, HD // 2, 1) * sine)
        return jnp.concatenate(outs, axis=1)

    def project(here, stream):
        def product(j):
            return jnp.dot(modded[here, :], weight[3 * stream + j], preferred_element_type=F32)

        cosine, sine = cos_ref[here, :], sin_ref[here, :]
        q = prepare(product(0), gain_ref[0:1, :], cosine, sine)
        q_ref[here, :] = (q * (math.log2(math.e) / math.sqrt(HD))).astype(BF)
        kv_ref[0, here, :] = prepare(product(1), gain_ref[1:2, :], cosine, sine).astype(BF)
        kv_ref[1, here, :] = product(2).astype(BF)

    image_copy.wait()
    for copy in w_copies[0]:
        copy.wait()
    chunk = image_rows // 2

    @pl.loop(0, 2)
    def _(step):
        project(pl.ds(pl.multiple_of(step * chunk, chunk), chunk), 0)

    for copy in w_copies[1]:
        copy.wait()
    project(pl.ds(image_rows, rows - image_rows), 1)


def qkv(image, text_a, w_pieces, w_places, mod, cosine, sine, gains):
    parts, text_rows, share = text_a.shape
    image_rows, width = image.shape
    rows = image_rows + text_rows
    count = len(w_pieces)
    return pl.pallas_call(
        functools.partial(qkv_kernel, count),
        out_shape=(
            jax.ShapeDtypeStruct((rows, share), BF),
            jax.ShapeDtypeStruct((2, rows, share), BF),
        ),
        in_specs=[SMEM, VMEM, VMEM, VMEM, VMEM] + [ANY] * (2 + count),
        out_specs=(VMEM, VMEM),
        scratch_shapes=[
            pltpu.VMEM((parts, text_rows, share), BF),
            pltpu.VMEM((rows, width), BF),
            pltpu.VMEM((6, width, share), BF),
            pltpu.SemaphoreType.DMA((2 * count + 2,)),
        ],
        compiler_params=params(),
        name="qkv",
    )(table(w_places), mod, cosine, sine, gains, image, text_a, *w_pieces)


def attention_kernel(nq, k_sizes, first, *refs):
    nk = len(k_sizes)
    q_refs, refs = refs[:nq], refs[nq:]
    k_refs, v_refs, refs = refs[:nk], refs[nk : 2 * nk], refs[2 * nk :]
    before, refs = ([], refs) if first else (refs[: 2 * nq], refs[2 * nq :])
    out_refs, tot_refs = refs[:nq], refs[nq : 2 * nq]
    keys, values = refs[2 * nq :]
    head = pl.program_id(0)
    at = 0
    for k_ref, v_ref, size in zip(k_refs, v_refs, k_sizes):
        keys[at : at + size, :] = k_ref[0]
        values[at : at + size, 0:HD] = v_ref[0]
        at += size

    @pl.when(head == 0)
    def _():
        values[:, HD:] = jnp.ones((values.shape[0], HD), BF)
        for i in range(nq):
            tot_refs[i][...] = jnp.zeros(tot_refs[i].shape, F32) if first else before[nq + i][...]

    rows = q_refs[0].shape[0]
    lane = lax.broadcasted_iota(jnp.int32, (rows, HD), 1)
    block = 256
    for i in range(nq):
        q = q_refs[i][...]
        total = jnp.zeros((rows, 2 * HD), F32)
        for start in range(0, keys.shape[0], block):
            stop = min(start + block, keys.shape[0])
            scores = lax.dot_general(
                q, keys[start:stop, :], (((1,), (1,)), ((), ())), preferred_element_type=F32
            )
            probs = jnp.exp2(scores).astype(BF)
            total += jnp.dot(probs, values[start:stop, :], preferred_element_type=F32)
        num = total[:, :HD]
        out_refs[i][...] = num if first else before[i][...] + num
        tot_refs[i][...] += jnp.where(lane == head, total[:, HD:], 0.0)


def attention(queries, kvs, before=()):
    rows, width = queries[0].shape
    keys = [(kv[0].reshape(-1, rows, width), 0) for kv in kvs]
    values = [(kv[-1].reshape(-1, rows, width), 2 - len(kv)) for kv in kvs]
    k_sizes = (rows,) * len(kvs)
    nq = len(queries)
    by_head = pl.BlockSpec((rows, HD), lambda h: (0, h))
    fixed = pl.BlockSpec((rows, HD), lambda h: (0, 0))
    sums = [by_head] * nq + [fixed] * nq
    inputs = nq + 2 * len(kvs)
    work = nq * rows * len(kvs) * rows * width
    return pl.pallas_call(
        functools.partial(attention_kernel, nq, k_sizes, not before),
        grid=(width // HD,),
        out_shape=[jax.ShapeDtypeStruct((rows, width), F32)] * nq
        + [jax.ShapeDtypeStruct((rows, HD), F32)] * nq,
        in_specs=[by_head] * nq
        + [
            pl.BlockSpec((1, rows, HD), functools.partial(lambda i, h: (i, 0, h), i))
            for _, i in keys + values
        ]
        + (sums if before else []),
        out_specs=sums,
        input_output_aliases={inputs + i: i for i in range(2 * nq)} if before else {},
        scratch_shapes=[
            pltpu.VMEM((sum(k_sizes), HD), BF),
            pltpu.VMEM((sum(k_sizes), 2 * HD), BF),
        ],
        compiler_params=params(),
        cost_estimate=pl.CostEstimate(
            flops=8 * work, bytes_accessed=8 * nq * rows * width, transcendentals=work // HD
        ),
        name="attention",
    )(*queries, *[k for k, _ in keys + values], *before)


def combine_kernel(num_ref, other_ref, back_ref, tot_ref, other_tot_ref, out_ref):
    share = num_ref.shape[1]
    for h in range(share // HD):
        cols = slice(h * HD, (h + 1) * HD)
        lane, low = slice(share + h, share + h + 1), slice(share + 64 + h, share + 65 + h)
        num = num_ref[:, cols] + other_ref[:, cols] + back_ref[:, cols].astype(F32)
        tot = tot_ref[:, h : h + 1] + other_tot_ref[:, h : h + 1]
        tot += back_ref[:, lane].astype(F32) + back_ref[:, low].astype(F32)
        out_ref[:, cols] = (num / tot).astype(BF)


def combine(num, other, back, tot, other_tot):
    return pl.pallas_call(
        combine_kernel,
        out_shape=jax.ShapeDtypeStruct(num.shape, BF),
        in_specs=[VMEM] * 5,
        out_specs=VMEM,
        compiler_params=params(),
        name="combine",
    )(num, other, back, tot, other_tot)


def out_kernel(place_ref, own_ref, other_ref, weight_ref, out_ref, attended):
    rows, share = own_ref.shape
    image_rows = rows // 5 * 4

    @pl.when(pl.program_id(0) == 0)
    def _():
        first = place_ref[0] == 0
        attended[:, :share] = jnp.where(first, own_ref[...], other_ref[...])
        attended[:, share:] = jnp.where(first, other_ref[...], own_ref[...])

    for stream, here in ((0, slice(0, image_rows)), (1, slice(image_rows, rows))):
        halves = [weight_ref[2 * y : 2 * y + 2, stream].reshape(share, share) for y in range(2)]
        out_ref[0, here, :] = lax.dot_general(
            attended[here, :],
            jnp.concatenate(halves, axis=1),
            (((1,), (1,)), ((), ())),
            preferred_element_type=F32,
        ).astype(BF)


def out_projection(own, other, weight, yl):
    rows, share = own.shape
    whole = pl.BlockSpec((rows, share), lambda x: (0, 0))
    return pl.pallas_call(
        out_kernel,
        grid=(4,),
        out_shape=jax.ShapeDtypeStruct((4, rows, share), BF),
        in_specs=[SMEM, whole, whole]
        + [pl.BlockSpec((4,) + weight.shape[1:], lambda x: (x, 0, 0, 0))],
        out_specs=pl.BlockSpec((1, rows, share), lambda x: (x, 0, 0)),
        scratch_shapes=[pltpu.VMEM((rows, 2 * share), BF)],
        compiler_params=params(),
        name="out_projection",
    )(table([yl]), own, other, weight)


def angles_of(positions):
    freqs = 10000.0 ** (-(jnp.arange(HD // 2, dtype=F32) * 2.0) / HD)
    angles = positions[:, None] * freqs[None, :]
    cosine, sine = jnp.cos(angles), jnp.sin(angles)
    return jnp.concatenate([cosine, cosine], axis=1), jnp.concatenate([-sine, sine], axis=1)


def shards(
    cond_hidden,
    cond_down,
    cond_resid,
    cond_gain,
    text_proj,
    image_states,
    image_mod,
    text_mod,
    query_gain,
    key_gain,
    image_qkv,
    text_qkv,
    image_out,
    text_out,
    cond_pos,
    image_cache,
    text_cache,
):
    seq_index = lax.axis_index(SEQ)
    tp_index = lax.axis_index(TP)
    image_rows, share = image_states.shape
    text_rows = cond_hidden.shape[0]

    yh, z, c, x, yl = (lax.axis_index(a) for a in AXES)
    together = lax.optimization_barrier
    outs = jnp.stack([jnp.transpose(image_out), jnp.transpose(text_out)])
    weight = jnp.transpose(jnp.concatenate([image_qkv, text_qkv], axis=1), (1, 0, 2))

    a_pair = shift(image_states, "yl", 1)
    a_near = near(image_states, "x")
    w_pair = shift(weight, "yh", 1)
    cond_hidden, a_pair, a_near = together((cond_hidden, a_pair, a_near))

    w_near = near(weight, "z")
    a_next = near(a_pair, "x")
    partial_value = jnp.dot(cond_hidden, cond_down, preferred_element_type=F32).astype(BF)
    enc_share = cond_down.shape[1] // 8
    sent = jnp.transpose(partial_value.reshape(text_rows, 8, enc_share), (1, 0, 2))
    got = lax.all_to_all(sent, TP, split_axis=0, concat_axis=0, tiled=True)
    got, a_near, a_next, w_near, w_pair, outs = together(
        (got, a_near, a_next, w_near, w_pair, outs)
    )

    a_far = (shift(a_near[0], "x", 1), shift(a_next[1], "x", -1))
    w_next = near(w_pair, "z")
    turned = [
        (4 * zh + 2 * zl + y, 4 * zh + 2 * y + zl)
        for zh in range(2)
        for zl in range(2)
        for y in range(2)
    ]
    outs = lax.ppermute(outs, ("z", "yl"), turned)
    out_w = lax.all_gather(outs, SEQ)
    cond_state = (jnp.sum(got.astype(F32), axis=0) + cond_resid.astype(F32)).astype(BF)
    state = spread(cond_state, TP)
    state, a_far, w_near, w_next, outs = together((state, a_far, w_near, w_next, outs))

    text_states = text_projection(state, cond_gain, text_proj)
    text_a = spread(text_states, TP)
    w_far = (shift(w_near[0], "z", 1), shift(w_next[1], "z", -1))

    blocks = [(p, d) for p in range(2) for d in (0, 3, 1, 2)]
    a_arrays = [image_states, *a_near, a_far[0], a_pair, *a_next, a_far[1]]
    a_places = [(x + d) % 4 * 2 + (yl + p) % 2 for p, d in blocks]
    image_modded = modulate(a_arrays, a_places, image_mod)
    text_a, w_far, image_modded = together((text_a, w_far, image_modded))

    w_arrays = [weight, *w_near, w_far[0], w_pair, *w_next, w_far[1]]
    w_arrays += [shift(w, "c", 1) for w in w_arrays]

    gains = jnp.stack([query_gain, key_gain])
    image_pos = (seq_index * image_rows + jnp.arange(image_rows)).astype(F32)
    w_places = [
        (yh + p) % 2 * 8 + (z + d) % 4 * 2 + (c + k) % 2 for k in range(2) for p, d in blocks
    ]
    query, kv = qkv(
        image_modded,
        text_a,
        w_arrays,
        w_places,
        text_mod,
        *angles_of(jnp.concatenate([image_pos, cond_pos.astype(F32)])),
        gains,
    )
    pair_query = shift(query, "yh", 1)
    kv_left, kv_right = near(kv, "z")
    core_query = shift(query, "c", 1)
    own_queries = [query, core_query]
    own = attention(own_queries, [(kv,)])
    pair_query, own = together((pair_query, own))
    pair_queries = [pair_query, shift(pair_query, "c", 1)]
    pair = attention(pair_queries, [(kv,)])
    pair, kv_left, kv_right = together((pair, kv_left, kv_right))
    kv_far = (shift(kv_left[0], "z", 1), shift(kv_right[1], "z", -1))
    pair = attention(pair_queries, [(kv_left,), (kv_right,)], pair)
    pair, kv_far = together((pair, kv_far))
    pair = attention(pair_queries, [kv_far], pair)

    sent_num = pair[0] + shift(pair[1], "c", 1)
    sent_tot = pair[2] + shift(pair[3], "c", 1)
    high = sent_tot.astype(BF)
    low = (sent_tot - high.astype(F32)).astype(BF)
    mixed = jnp.concatenate([sent_num.astype(BF), high[:, :64], low[:, :64]], axis=1)
    mixed, own = together((mixed, own))
    back = shift(mixed, "yh", 1)
    own = attention(own_queries, [(kv_left,), (kv_right,), kv_far], own)
    back, own = together((back, own))
    attended = combine(own[0], shift(own[1], "c", 1), back, own[2], shift(own[3], "c", 1))

    parts = out_projection(attended, shift(attended, "yl", 1), out_w, yl)
    got = lax.all_to_all(parts, "x", split_axis=0, concat_axis=0, tiled=True)
    branch = jnp.sum(got.astype(F32), axis=0)

    def finish(states, mod, rows, cache):
        gates = lax.dynamic_slice_in_dim(mod, tp_index * share, share, 1)
        return (
            states.astype(F32) + gates[2] * branch[rows] + gates[3] * cache.astype(F32)
        ).astype(BF)

    return (
        finish(image_states, image_mod, slice(0, image_rows), image_cache),
        finish(text_states, text_mod, slice(image_rows, None), text_cache),
    )


def solution(mesh):
    fine = Mesh(mesh.devices.reshape(2, 4, 2, 4, 2), AXES)
    return jax.shard_map(
        shards,
        mesh=fine,
        in_specs=(
            P(SEQ, TP),
            P(TP, None),
            P(SEQ, TP),
            P(),
            P(None, TP),
            P(SEQ, TP),
            P(),
            P(),
            P(),
            P(),
            P(SEQ, None, TP),
            P(SEQ, None, TP),
            P(TP, SEQ),
            P(TP, SEQ),
            P(SEQ),
            P(SEQ, TP),
            P(SEQ, TP),
        ),
        out_specs=(P(SEQ, TP), P(SEQ, TP)),
        check_vma=False,
    )
```

```python
import functools
import math

import jax
import jax.numpy as jnp
from jax import lax
from jax.experimental import pallas as pl
from jax.experimental.pallas import tpu as pltpu
from jax.sharding import Mesh, PartitionSpec as P

EPS = 1e-06
HD = 128
AXES = ("yh", "z", "c", "x", "yl")
SEQ = ("yh", "z", "c")
TP = ("x", "yl")
BF = jnp.bfloat16
F32 = jnp.float32


def shift(value, axis, step):
    size = lax.axis_size(axis)
    return lax.ppermute(value, axis, [(k, (k + step) % size) for k in range(size)])


def near(value, axis):
    return shift(value, axis, 1), shift(value, axis, -1)


def spread(value, axes):
    count = lax.axis_size(axes)
    copies = jnp.broadcast_to(value[None], (count,) + value.shape)
    return lax.all_to_all(copies, axes, split_axis=0, concat_axis=0, tiled=True)


def table(places):
    return jnp.stack([jnp.asarray(p, jnp.int32) for p in places])


def params(mib):
    return pltpu.CompilerParams(vmem_limit_bytes=mib * 1024 * 1024)


ANY = pl.BlockSpec(memory_space=pl.ANY)
VMEM = pl.BlockSpec(memory_space=pltpu.VMEM)
SMEM = pl.BlockSpec(memory_space=pltpu.SMEM)


def text_kernel(state_ref, gain_ref, proj_ref, out_ref):
    parts, rows, share = state_ref.shape
    square = jnp.zeros((rows, 1), F32)
    for t in range(parts):
        block = state_ref[t].astype(F32)
        square += jnp.sum(block * block, axis=-1, keepdims=True)
    factor = lax.rsqrt(square / (parts * share) + EPS)
    total = jnp.zeros(out_ref.shape, F32)
    for t in range(parts):
        normed = (state_ref[t].astype(F32) * factor * gain_ref[t]).astype(BF)
        total += jnp.dot(normed, proj_ref[t], preferred_element_type=F32)
    out_ref[...] = total.astype(BF)


def text_projection(state, gain, proj):
    parts, rows, share = state.shape
    return pl.pallas_call(
        text_kernel,
        out_shape=jax.ShapeDtypeStruct((rows, proj.shape[1]), BF),
        in_specs=[VMEM] * 3,
        out_specs=VMEM,
        compiler_params=params(16),
        name="text_projection",
    )(state, gain.reshape(parts, 1, share), proj.reshape(parts, share, proj.shape[1]))


def normalise(states, mod_ref, out_ref, first):
    parts, rows, share = states.shape
    width = parts * share
    tile = 64

    @pl.loop(0, rows // tile)
    def _(step):
        here = pl.ds(pl.multiple_of(step * tile, tile), tile)
        there = pl.ds(pl.multiple_of(first + step * tile, tile), tile)
        total = jnp.zeros((tile, share), F32)
        for t in range(parts):
            total += states[t, here, :].astype(F32)
        center = jnp.sum(total, axis=-1, keepdims=True) / width
        total = jnp.zeros((tile, share), F32)
        for t in range(parts):
            shifted = states[t, here, :].astype(F32) - center
            total += shifted * shifted
        factor = lax.rsqrt(jnp.sum(total, axis=-1, keepdims=True) / width + EPS)
        for t in range(parts):
            cols = slice(t * share, (t + 1) * share)
            shifted = states[t, here, :].astype(F32) - center
            normed = shifted * factor * (1.0 + mod_ref[1:2, cols]) + mod_ref[0:1, cols]
            out_ref[there, cols] = normed.astype(BF)


def modulate_kernel(count, place_ref, mod_ref, *refs):
    pieces, (out_ref, states, sems) = refs[:count], refs[count:]
    copies = [
        pltpu.make_async_copy(piece, states.at[place_ref[i]], sems.at[i])
        for i, piece in enumerate(pieces)
    ]
    for copy in copies:
        copy.start()
    for copy in copies:
        copy.wait()
    normalise(states, mod_ref, out_ref, 0)


def modulate(pieces, places, mod):
    rows, share = pieces[0].shape
    count = len(pieces)
    return pl.pallas_call(
        functools.partial(modulate_kernel, count),
        out_shape=jax.ShapeDtypeStruct((rows, count * share), BF),
        in_specs=[SMEM, VMEM] + [ANY] * count,
        out_specs=VMEM,
        scratch_shapes=[
            pltpu.VMEM((count, rows, share), BF),
            pltpu.SemaphoreType.DMA((count,)),
        ],
        compiler_params=params(16),
        name="modulate",
    )(table(places), mod, *pieces)


def qkv_kernel(count, place_ref, mod_ref, cos_ref, sin_ref, gain_ref, image_ref, *refs):
    text_ref, w_pieces, refs = refs[0], refs[1 : 1 + count], refs[1 + count :]
    q_ref, kv_ref, states, modded, weight, sems = refs
    share = states.shape[2]
    rows, width = modded.shape
    depth = width // 16
    image_rows = image_ref.shape[0]
    image_copy = pltpu.make_async_copy(
        image_ref, modded.at[pl.ds(0, image_rows)], sems.at[2 * count]
    )
    text_copy = pltpu.make_async_copy(text_ref, states, sems.at[2 * count + 1])
    w_copies = ([], [])
    for stream in range(2):
        for i, piece in enumerate(w_pieces):
            start = pl.multiple_of(place_ref[i] * depth, depth)
            src = piece.at[pl.ds(3 * stream, 3)]
            dst = weight.at[pl.ds(3 * stream, 3), pl.ds(start, depth), :]
            sem = sems.at[count * stream + i]
            w_copies[stream].append(pltpu.make_async_copy(src, dst, sem))
    for copy in [text_copy, image_copy] + w_copies[0] + w_copies[1]:
        copy.start()
    text_copy.wait()
    normalise(states, mod_ref, modded, image_rows)

    def prepare(flat, gain, cosine, sine):
        outs = []
        for h in range(share // HD):
            head = flat[:, h * HD : (h + 1) * HD]
            meansq = jnp.mean(head * head, axis=-1, keepdims=True)
            normed = head * lax.rsqrt(meansq + EPS) * gain
            outs.append(normed * cosine + pltpu.roll(normed, HD // 2, 1) * sine)
        return jnp.concatenate(outs, axis=1)

    def project(here, stream):
        def product(j):
            return jnp.dot(modded[here, :], weight[3 * stream + j], preferred_element_type=F32)

        cosine, sine = cos_ref[here, :], sin_ref[here, :]
        q = prepare(product(0), gain_ref[0:1, :], cosine, sine)
        q_ref[here, :] = (q * (math.log2(math.e) / math.sqrt(HD))).astype(BF)
        kv_ref[0, here, :] = prepare(product(1), gain_ref[1:2, :], cosine, sine).astype(BF)
        kv_ref[1, here, :] = product(2).astype(BF)

    image_copy.wait()
    for copy in w_copies[0]:
        copy.wait()
    chunk = image_rows // 2

    @pl.loop(0, 2)
    def _(step):
        project(pl.ds(pl.multiple_of(step * chunk, chunk), chunk), 0)

    for copy in w_copies[1]:
        copy.wait()
    project(pl.ds(image_rows, rows - image_rows), 1)


def qkv(image, text_a, w_pieces, w_places, mod, cosine, sine, gains):
    parts, text_rows, share = text_a.shape
    image_rows, width = image.shape
    rows = image_rows + text_rows
    count = len(w_pieces)
    return pl.pallas_call(
        functools.partial(qkv_kernel, count),
        out_shape=(
            jax.ShapeDtypeStruct((rows, share), BF),
            jax.ShapeDtypeStruct((2, rows, share), BF),
        ),
        in_specs=[SMEM, VMEM, VMEM, VMEM, VMEM] + [ANY] * (2 + count),
        out_specs=(VMEM, VMEM),
        scratch_shapes=[
            pltpu.VMEM((parts, text_rows, share), BF),
            pltpu.VMEM((rows, width), BF),
            pltpu.VMEM((6, width, share), BF),
            pltpu.SemaphoreType.DMA((2 * count + 2,)),
        ],
        compiler_params=params(36),
        name="qkv",
    )(table(w_places), mod, cosine, sine, gains, image, text_a, *w_pieces)


def attention_kernel(nq, k_sizes, first, *refs):
    nk = len(k_sizes)
    q_refs, refs = refs[:nq], refs[nq:]
    k_refs, v_refs, refs = refs[:nk], refs[nk : 2 * nk], refs[2 * nk :]
    before, refs = ([], refs) if first else (refs[: 2 * nq], refs[2 * nq :])
    out_refs, tot_refs = refs[:nq], refs[nq : 2 * nq]
    keys, values = refs[2 * nq :]
    head = pl.program_id(0)
    at = 0
    for k_ref, v_ref, size in zip(k_refs, v_refs, k_sizes):
        keys[at : at + size, :] = k_ref[0]
        values[at : at + size, 0:HD] = v_ref[0]
        at += size

    @pl.when(head == 0)
    def _():
        values[:, HD:] = jnp.ones((values.shape[0], HD), BF)
        for i in range(nq):
            tot_refs[i][...] = jnp.zeros(tot_refs[i].shape, F32) if first else before[nq + i][...]

    rows = q_refs[0].shape[0]
    lane = lax.broadcasted_iota(jnp.int32, (rows, HD), 1)
    block = 256
    for i in range(nq):
        q = q_refs[i][...]
        total = jnp.zeros((rows, 2 * HD), F32)
        for start in range(0, keys.shape[0], block):
            stop = min(start + block, keys.shape[0])
            scores = lax.dot_general(
                q, keys[start:stop, :], (((1,), (1,)), ((), ())), preferred_element_type=F32
            )
            probs = jnp.exp2(scores).astype(BF)
            total += jnp.dot(probs, values[start:stop, :], preferred_element_type=F32)
        num = total[:, :HD]
        out_refs[i][...] = num if first else before[i][...] + num
        tot_refs[i][...] += jnp.where(lane == head, total[:, HD:], 0.0)


def attention(queries, kvs, before=()):
    rows, width = queries[0].shape
    keys = [(kv[0].reshape(-1, rows, width), 0) for kv in kvs]
    values = [(kv[-1].reshape(-1, rows, width), 2 - len(kv)) for kv in kvs]
    k_sizes = (rows,) * len(kvs)
    nq = len(queries)
    by_head = pl.BlockSpec((rows, HD), lambda h: (0, h))
    fixed = pl.BlockSpec((rows, HD), lambda h: (0, 0))
    sums = [by_head] * nq + [fixed] * nq
    inputs = nq + 2 * len(kvs)
    work = nq * rows * len(kvs) * rows * width
    return pl.pallas_call(
        functools.partial(attention_kernel, nq, k_sizes, not before),
        grid=(width // HD,),
        out_shape=[jax.ShapeDtypeStruct((rows, width), F32)] * nq
        + [jax.ShapeDtypeStruct((rows, HD), F32)] * nq,
        in_specs=[by_head] * nq
        + [
            pl.BlockSpec((1, rows, HD), functools.partial(lambda i, h: (i, 0, h), i))
            for _, i in keys + values
        ]
        + (sums if before else []),
        out_specs=sums,
        input_output_aliases={inputs + i: i for i in range(2 * nq)} if before else {},
        scratch_shapes=[
            pltpu.VMEM((sum(k_sizes), HD), BF),
            pltpu.VMEM((sum(k_sizes), 2 * HD), BF),
        ],
        compiler_params=params(24),
        cost_estimate=pl.CostEstimate(
            flops=8 * work, bytes_accessed=8 * nq * rows * width, transcendentals=work // HD
        ),
        name="attention",
    )(*queries, *[k for k, _ in keys + values], *before)


def combine_kernel(num_ref, other_ref, back_ref, tot_ref, other_tot_ref, out_ref):
    share = num_ref.shape[1]
    for h in range(share // HD):
        cols = slice(h * HD, (h + 1) * HD)
        lane, low = slice(share + h, share + h + 1), slice(share + 64 + h, share + 65 + h)
        num = num_ref[:, cols] + other_ref[:, cols] + back_ref[:, cols].astype(F32)
        tot = tot_ref[:, h : h + 1] + other_tot_ref[:, h : h + 1]
        tot += back_ref[:, lane].astype(F32) + back_ref[:, low].astype(F32)
        out_ref[:, cols] = (num / tot).astype(BF)


def combine(num, other, back, tot, other_tot):
    return pl.pallas_call(
        combine_kernel,
        out_shape=jax.ShapeDtypeStruct(num.shape, BF),
        in_specs=[VMEM] * 5,
        out_specs=VMEM,
        compiler_params=params(16),
        name="combine",
    )(num, other, back, tot, other_tot)


def out_kernel(place_ref, own_ref, other_ref, weight_ref, out_ref, attended):
    rows, share = own_ref.shape
    image_rows = rows // 5 * 4

    @pl.when(pl.program_id(0) == 0)
    def _():
        first = place_ref[0] == 0
        attended[:, :share] = jnp.where(first, own_ref[...], other_ref[...])
        attended[:, share:] = jnp.where(first, other_ref[...], own_ref[...])

    for stream, here in ((0, slice(0, image_rows)), (1, slice(image_rows, rows))):
        halves = [weight_ref[2 * y : 2 * y + 2, stream].reshape(share, share) for y in range(2)]
        out_ref[0, here, :] = lax.dot_general(
            attended[here, :],
            jnp.concatenate(halves, axis=1),
            (((1,), (1,)), ((), ())),
            preferred_element_type=F32,
        ).astype(BF)


def out_projection(own, other, weight, yl):
    rows, share = own.shape
    whole = pl.BlockSpec((rows, share), lambda x: (0, 0))
    return pl.pallas_call(
        out_kernel,
        grid=(4,),
        out_shape=jax.ShapeDtypeStruct((4, rows, share), BF),
        in_specs=[SMEM, whole, whole]
        + [pl.BlockSpec((4,) + weight.shape[1:], lambda x: (x, 0, 0, 0))],
        out_specs=pl.BlockSpec((1, rows, share), lambda x: (x, 0, 0)),
        scratch_shapes=[pltpu.VMEM((rows, 2 * share), BF)],
        compiler_params=params(24),
        name="out_projection",
    )(table([yl]), own, other, weight)


def angles_of(positions):
    freqs = 10000.0 ** (-(jnp.arange(HD // 2, dtype=F32) * 2.0) / HD)
    angles = positions[:, None] * freqs[None, :]
    cosine, sine = jnp.cos(angles), jnp.sin(angles)
    return jnp.concatenate([cosine, cosine], axis=1), jnp.concatenate([-sine, sine], axis=1)


def shards(
    cond_hidden,
    cond_down,
    cond_resid,
    cond_gain,
    text_proj,
    image_states,
    image_mod,
    text_mod,
    query_gain,
    key_gain,
    image_qkv,
    text_qkv,
    image_out,
    text_out,
    cond_pos,
    image_cache,
    text_cache,
):
    seq_index = lax.axis_index(SEQ)
    tp_index = lax.axis_index(TP)
    image_rows, share = image_states.shape
    text_rows = cond_hidden.shape[0]

    yh, z, c, x, yl = (lax.axis_index(a) for a in AXES)
    together = lax.optimization_barrier
    outs = jnp.stack([jnp.transpose(image_out), jnp.transpose(text_out)])
    weight = jnp.transpose(jnp.concatenate([image_qkv, text_qkv], axis=1), (1, 0, 2))

    a_pair = shift(image_states, "yl", 1)
    a_near = near(image_states, "x")
    w_pair = shift(weight, "yh", 1)
    cond_hidden, a_pair, a_near = together((cond_hidden, a_pair, a_near))

    w_near = near(weight, "z")
    a_next = near(a_pair, "x")
    partial_value = jnp.dot(cond_hidden, cond_down, preferred_element_type=F32).astype(BF)
    enc_share = cond_down.shape[1] // 8
    sent = jnp.transpose(partial_value.reshape(text_rows, 8, enc_share), (1, 0, 2))
    got = lax.all_to_all(sent, TP, split_axis=0, concat_axis=0, tiled=True)
    got, a_near, a_next, w_near, w_pair, outs = together(
        (got, a_near, a_next, w_near, w_pair, outs)
    )

    a_far = (shift(a_near[0], "x", 1), shift(a_next[1], "x", -1))
    w_next = near(w_pair, "z")
    turned = [
        (4 * zh + 2 * zl + y, 4 * zh + 2 * y + zl)
        for zh in range(2)
        for zl in range(2)
        for y in range(2)
    ]
    outs = lax.ppermute(outs, ("z", "yl"), turned)
    out_w = lax.all_gather(outs, SEQ)
    cond_state = (jnp.sum(got.astype(F32), axis=0) + cond_resid.astype(F32)).astype(BF)
    state = spread(cond_state, TP)
    state, a_far, w_near, w_next, outs = together((state, a_far, w_near, w_next, outs))

    text_states = text_projection(state, cond_gain, text_proj)
    text_a = spread(text_states, TP)
    w_far = (shift(w_near[0], "z", 1), shift(w_next[1], "z", -1))

    blocks = [(p, d) for p in range(2) for d in (0, 3, 1, 2)]
    a_arrays = [image_states, *a_near, a_far[0], a_pair, *a_next, a_far[1]]
    a_places = [(x + d) % 4 * 2 + (yl + p) % 2 for p, d in blocks]
    image_modded = modulate(a_arrays, a_places, image_mod)
    text_a, w_far, image_modded = together((text_a, w_far, image_modded))

    w_arrays = [weight, *w_near, w_far[0], w_pair, *w_next, w_far[1]]
    w_arrays += [shift(w, "c", 1) for w in w_arrays]

    gains = jnp.stack([query_gain, key_gain])
    image_pos = (seq_index * image_rows + jnp.arange(image_rows)).astype(F32)
    w_places = [
        (yh + p) % 2 * 8 + (z + d) % 4 * 2 + (c + k) % 2 for k in range(2) for p, d in blocks
    ]
    query, kv = qkv(
        image_modded,
        text_a,
        w_arrays,
        w_places,
        text_mod,
        *angles_of(jnp.concatenate([image_pos, cond_pos.astype(F32)])),
        gains,
    )
    pair_query = shift(query, "yh", 1)
    kv_left, kv_right = near(kv, "z")
    core_query = shift(query, "c", 1)
    own_queries = [query, core_query]
    own = attention(own_queries, [(kv,)])
    pair_query, own = together((pair_query, own))
    pair_queries = [pair_query, shift(pair_query, "c", 1)]
    pair = attention(pair_queries, [(kv,)])
    pair, kv_left, kv_right = together((pair, kv_left, kv_right))
    kv_far = (shift(kv_left[0], "z", 1), shift(kv_right[1], "z", -1))
    pair = attention(pair_queries, [(kv_left,), (kv_right,)], pair)
    pair, kv_far = together((pair, kv_far))
    pair = attention(pair_queries, [kv_far], pair)

    sent_num = pair[0] + shift(pair[1], "c", 1)
    sent_tot = pair[2] + shift(pair[3], "c", 1)
    high = sent_tot.astype(BF)
    low = (sent_tot - high.astype(F32)).astype(BF)
    mixed = jnp.concatenate([sent_num.astype(BF), high[:, :64], low[:, :64]], axis=1)
    mixed, own = together((mixed, own))
    back = shift(mixed, "yh", 1)
    own = attention(own_queries, [(kv_left,), (kv_right,), kv_far], own)
    back, own = together((back, own))
    attended = combine(own[0], shift(own[1], "c", 1), back, own[2], shift(own[3], "c", 1))

    parts = out_projection(attended, shift(attended, "yl", 1), out_w, yl)
    got = lax.all_to_all(parts, "x", split_axis=0, concat_axis=0, tiled=True)
    branch = jnp.sum(got.astype(F32), axis=0)

    def finish(states, mod, rows, cache):
        gates = lax.dynamic_slice_in_dim(mod, tp_index * share, share, 1)
        return (
            states.astype(F32) + gates[2] * branch[rows] + gates[3] * cache.astype(F32)
        ).astype(BF)

    return (
        finish(image_states, image_mod, slice(0, image_rows), image_cache),
        finish(text_states, text_mod, slice(image_rows, None), text_cache),
    )


def solution(mesh):
    fine = Mesh(mesh.devices.reshape(2, 4, 2, 4, 2), AXES)
    return jax.shard_map(
        shards,
        mesh=fine,
        in_specs=(
            P(SEQ, TP),
            P(TP, None),
            P(SEQ, TP),
            P(),
            P(None, TP),
            P(SEQ, TP),
            P(),
            P(),
            P(),
            P(),
            P(SEQ, None, TP),
            P(SEQ, None, TP),
            P(TP, SEQ),
            P(TP, SEQ),
            P(SEQ),
            P(SEQ, TP),
            P(SEQ, TP),
        ),
        out_specs=(P(SEQ, TP), P(SEQ, TP)),
        check_vma=False,
    )
```

```python
import functools
import math

import jax
import jax.numpy as jnp
from jax import lax
from jax.experimental import pallas as pl
from jax.experimental.pallas import tpu as pltpu
from jax.sharding import Mesh, PartitionSpec as P

EPS = 1e-06
HD = 128
AXES = ("yh", "z", "c", "x", "yl")
SEQ = ("yh", "z", "c")
TP = ("x", "yl")
BF = jnp.bfloat16
F32 = jnp.float32


def shift(value, axis, step):
    size = lax.axis_size(axis)
    return lax.ppermute(value, axis, [(k, (k + step) % size) for k in range(size)])


def near(value, axis):
    return shift(value, axis, 1), shift(value, axis, -1)


def spread(value, axes):
    count = lax.axis_size(axes)
    copies = jnp.broadcast_to(value[None], (count,) + value.shape)
    return lax.all_to_all(copies, axes, split_axis=0, concat_axis=0, tiled=True)


def table(places):
    return jnp.stack([jnp.asarray(p, jnp.int32) for p in places])


def params(mib):
    return pltpu.CompilerParams(vmem_limit_bytes=mib * 1024 * 1024)


ANY = pl.BlockSpec(memory_space=pl.ANY)
VMEM = pl.BlockSpec(memory_space=pltpu.VMEM)
SMEM = pl.BlockSpec(memory_space=pltpu.SMEM)


def text_kernel(state_ref, gain_ref, proj_ref, out_ref):
    parts, rows, share = state_ref.shape
    square = jnp.zeros((rows, 1), F32)
    for t in range(parts):
        block = state_ref[t].astype(F32)
        square += jnp.sum(block * block, axis=-1, keepdims=True)
    factor = lax.rsqrt(square / (parts * share) + EPS)
    total = jnp.zeros(out_ref.shape, F32)
    for t in range(parts):
        normed = (state_ref[t].astype(F32) * factor * gain_ref[t]).astype(BF)
        total += jnp.dot(normed, proj_ref[t], preferred_element_type=F32)
    out_ref[...] = total.astype(BF)


def text_projection(state, gain, proj):
    parts, rows, share = state.shape
    return pl.pallas_call(
        text_kernel,
        out_shape=jax.ShapeDtypeStruct((rows, proj.shape[1]), BF),
        in_specs=[VMEM] * 3,
        out_specs=VMEM,
        compiler_params=params(16),
        name="text_projection",
    )(state, gain.reshape(parts, 1, share), proj.reshape(parts, share, proj.shape[1]))


def normalise(states, mod_ref, out_ref, first):
    parts, rows, share = states.shape
    width = parts * share
    tile = 64

    @pl.loop(0, rows // tile)
    def _(step):
        here = pl.ds(pl.multiple_of(step * tile, tile), tile)
        there = pl.ds(pl.multiple_of(first + step * tile, tile), tile)
        total = jnp.zeros((tile, share), F32)
        for t in range(parts):
            total += states[t, here, :].astype(F32)
        center = jnp.sum(total, axis=-1, keepdims=True) / width
        total = jnp.zeros((tile, share), F32)
        for t in range(parts):
            shifted = states[t, here, :].astype(F32) - center
            total += shifted * shifted
        factor = lax.rsqrt(jnp.sum(total, axis=-1, keepdims=True) / width + EPS)
        for t in range(parts):
            cols = slice(t * share, (t + 1) * share)
            shifted = states[t, here, :].astype(F32) - center
            normed = shifted * factor * (1.0 + mod_ref[1:2, cols]) + mod_ref[0:1, cols]
            out_ref[there, cols] = normed.astype(BF)


def modulate_kernel(count, place_ref, mod_ref, *refs):
    pieces, (out_ref, states, sems) = refs[:count], refs[count:]
    copies = [
        pltpu.make_async_copy(piece, states.at[place_ref[i]], sems.at[i])
        for i, piece in enumerate(pieces)
    ]
    for copy in copies:
        copy.start()
    for copy in copies:
        copy.wait()
    normalise(states, mod_ref, out_ref, 0)


def modulate(pieces, places, mod):
    rows, share = pieces[0].shape
    count = len(pieces)
    return pl.pallas_call(
        functools.partial(modulate_kernel, count),
        out_shape=jax.ShapeDtypeStruct((rows, count * share), BF),
        in_specs=[SMEM, VMEM] + [ANY] * count,
        out_specs=VMEM,
        scratch_shapes=[
            pltpu.VMEM((count, rows, share), BF),
            pltpu.SemaphoreType.DMA((count,)),
        ],
        compiler_params=params(16),
        name="modulate",
    )(table(places), mod, *pieces)


def qkv_kernel(count, place_ref, mod_ref, cos_ref, sin_ref, gain_ref, image_ref, *refs):
    text_ref, w_pieces, refs = refs[0], refs[1 : 1 + count], refs[1 + count :]
    q_ref, kv_ref, states, modded, weight, sems = refs
    share = states.shape[2]
    rows, width = modded.shape
    depth = width // 16
    image_rows = image_ref.shape[0]
    image_copy = pltpu.make_async_copy(
        image_ref, modded.at[pl.ds(0, image_rows)], sems.at[2 * count]
    )
    text_copy = pltpu.make_async_copy(text_ref, states, sems.at[2 * count + 1])
    w_copies = ([], [])
    for stream in range(2):
        for i, piece in enumerate(w_pieces):
            start = pl.multiple_of(place_ref[i] * depth, depth)
            src = piece.at[pl.ds(3 * stream, 3)]
            dst = weight.at[pl.ds(3 * stream, 3), pl.ds(start, depth), :]
            sem = sems.at[count * stream + i]
            w_copies[stream].append(pltpu.make_async_copy(src, dst, sem))
    for copy in [text_copy, image_copy] + w_copies[0] + w_copies[1]:
        copy.start()
    text_copy.wait()
    normalise(states, mod_ref, modded, image_rows)

    def prepare(flat, gain, cosine, sine):
        outs = []
        for h in range(share // HD):
            head = flat[:, h * HD : (h + 1) * HD]
            meansq = jnp.mean(head * head, axis=-1, keepdims=True)
            normed = head * lax.rsqrt(meansq + EPS) * gain
            outs.append(normed * cosine + pltpu.roll(normed, HD // 2, 1) * sine)
        return jnp.concatenate(outs, axis=1)

    def project(here, stream):
        def product(j):
            return jnp.dot(modded[here, :], weight[3 * stream + j], preferred_element_type=F32)

        cosine, sine = cos_ref[here, :], sin_ref[here, :]
        q = prepare(product(0), gain_ref[0:1, :], cosine, sine)
        q_ref[here, :] = (q * (math.log2(math.e) / math.sqrt(HD))).astype(BF)
        kv_ref[0, here, :] = prepare(product(1), gain_ref[1:2, :], cosine, sine).astype(BF)
        kv_ref[1, here, :] = product(2).astype(BF)

    image_copy.wait()
    for copy in w_copies[0]:
        copy.wait()
    chunk = image_rows // 2

    @pl.loop(0, 2)
    def _(step):
        project(pl.ds(pl.multiple_of(step * chunk, chunk), chunk), 0)

    for copy in w_copies[1]:
        copy.wait()
    project(pl.ds(image_rows, rows - image_rows), 1)


def qkv(image, text_a, w_pieces, w_places, mod, cosine, sine, gains):
    parts, text_rows, share = text_a.shape
    image_rows, width = image.shape
    rows = image_rows + text_rows
    count = len(w_pieces)
    return pl.pallas_call(
        functools.partial(qkv_kernel, count),
        out_shape=(
            jax.ShapeDtypeStruct((rows, share), BF),
            jax.ShapeDtypeStruct((2, rows, share), BF),
        ),
        in_specs=[SMEM, VMEM, VMEM, VMEM, VMEM] + [ANY] * (2 + count),
        out_specs=(VMEM, VMEM),
        scratch_shapes=[
            pltpu.VMEM((parts, text_rows, share), BF),
            pltpu.VMEM((rows, width), BF),
            pltpu.VMEM((6, width, share), BF),
            pltpu.SemaphoreType.DMA((2 * count + 2,)),
        ],
        compiler_params=params(36),
        name="qkv",
    )(table(w_places), mod, cosine, sine, gains, image, text_a, *w_pieces)


def attention_kernel(nq, k_sizes, first, *refs):
    nk = len(k_sizes)
    q_refs, refs = refs[:nq], refs[nq:]
    k_refs, v_refs, refs = refs[:nk], refs[nk : 2 * nk], refs[2 * nk :]
    before, refs = ([], refs) if first else (refs[: 2 * nq], refs[2 * nq :])
    out_refs, tot_refs = refs[:nq], refs[nq : 2 * nq]
    keys, values = refs[2 * nq :]
    head = pl.program_id(0)
    at = 0
    for k_ref, v_ref, size in zip(k_refs, v_refs, k_sizes):
        keys[at : at + size, :] = k_ref[0]
        values[at : at + size, 0:HD] = v_ref[0]
        at += size

    @pl.when(head == 0)
    def _():
        values[:, HD:] = jnp.ones((values.shape[0], HD), BF)
        for i in range(nq):
            tot_refs[i][...] = jnp.zeros(tot_refs[i].shape, F32) if first else before[nq + i][...]

    rows = q_refs[0].shape[0]
    lane = lax.broadcasted_iota(jnp.int32, (rows, HD), 1)
    block = 256
    for i in range(nq):
        q = q_refs[i][...]
        total = jnp.zeros((rows, 2 * HD), F32)
        for start in range(0, keys.shape[0], block):
            stop = min(start + block, keys.shape[0])
            scores = lax.dot_general(
                q, keys[start:stop, :], (((1,), (1,)), ((), ())), preferred_element_type=F32
            )
            probs = jnp.exp2(scores).astype(BF)
            total += jnp.dot(probs, values[start:stop, :], preferred_element_type=F32)
        num = total[:, :HD]
        out_refs[i][...] = num if first else before[i][...] + num
        tot_refs[i][...] += jnp.where(lane == head, total[:, HD:], 0.0)


def attention(queries, kvs, before=()):
    rows, width = queries[0].shape
    keys = [(kv[0].reshape(-1, rows, width), 0) for kv in kvs]
    values = [(kv[-1].reshape(-1, rows, width), 2 - len(kv)) for kv in kvs]
    k_sizes = (rows,) * len(kvs)
    nq = len(queries)
    by_head = pl.BlockSpec((rows, HD), lambda h: (0, h))
    fixed = pl.BlockSpec((rows, HD), lambda h: (0, 0))
    sums = [by_head] * nq + [fixed] * nq
    inputs = nq + 2 * len(kvs)
    work = nq * rows * len(kvs) * rows * width
    return pl.pallas_call(
        functools.partial(attention_kernel, nq, k_sizes, not before),
        grid=(width // HD,),
        out_shape=[jax.ShapeDtypeStruct((rows, width), F32)] * nq
        + [jax.ShapeDtypeStruct((rows, HD), F32)] * nq,
        in_specs=[by_head] * nq
        + [
            pl.BlockSpec((1, rows, HD), functools.partial(lambda i, h: (i, 0, h), i))
            for _, i in keys + values
        ]
        + (sums if before else []),
        out_specs=sums,
        input_output_aliases={inputs + i: i for i in range(2 * nq)} if before else {},
        scratch_shapes=[
            pltpu.VMEM((sum(k_sizes), HD), BF),
            pltpu.VMEM((sum(k_sizes), 2 * HD), BF),
        ],
        compiler_params=params(24),
        cost_estimate=pl.CostEstimate(
            flops=8 * work, bytes_accessed=8 * nq * rows * width, transcendentals=work // HD
        ),
        name="attention",
    )(*queries, *[k for k, _ in keys + values], *before)


def combine_kernel(num_ref, other_ref, back_ref, tot_ref, other_tot_ref, out_ref):
    share = num_ref.shape[1]
    for h in range(share // HD):
        cols = slice(h * HD, (h + 1) * HD)
        lane, low = slice(share + h, share + h + 1), slice(share + 64 + h, share + 65 + h)
        num = num_ref[:, cols] + other_ref[:, cols] + back_ref[:, cols].astype(F32)
        tot = tot_ref[:, h : h + 1] + other_tot_ref[:, h : h + 1]
        tot += back_ref[:, lane].astype(F32) + back_ref[:, low].astype(F32)
        out_ref[:, cols] = (num / tot).astype(BF)


def combine(num, other, back, tot, other_tot):
    return pl.pallas_call(
        combine_kernel,
        out_shape=jax.ShapeDtypeStruct(num.shape, BF),
        in_specs=[VMEM] * 5,
        out_specs=VMEM,
        compiler_params=params(16),
        name="combine",
    )(num, other, back, tot, other_tot)


def out_kernel(place_ref, own_ref, other_ref, weight_ref, out_ref, attended):
    rows, share = own_ref.shape
    image_rows = rows // 5 * 4

    @pl.when(pl.program_id(0) == 0)
    def _():
        first = place_ref[0] == 0
        attended[:, :share] = jnp.where(first, own_ref[...], other_ref[...])
        attended[:, share:] = jnp.where(first, other_ref[...], own_ref[...])

    for stream, here in ((0, slice(0, image_rows)), (1, slice(image_rows, rows))):
        halves = [weight_ref[2 * y : 2 * y + 2, stream].reshape(share, share) for y in range(2)]
        out_ref[0, here, :] = lax.dot_general(
            attended[here, :],
            jnp.concatenate(halves, axis=1),
            (((1,), (1,)), ((), ())),
            preferred_element_type=F32,
        ).astype(BF)


def out_projection(own, other, weight, yl):
    rows, share = own.shape
    whole = pl.BlockSpec((rows, share), lambda x: (0, 0))
    return pl.pallas_call(
        out_kernel,
        grid=(4,),
        out_shape=jax.ShapeDtypeStruct((4, rows, share), BF),
        in_specs=[SMEM, whole, whole]
        + [pl.BlockSpec((4,) + weight.shape[1:], lambda x: (x, 0, 0, 0))],
        out_specs=pl.BlockSpec((1, rows, share), lambda x: (x, 0, 0)),
        scratch_shapes=[pltpu.VMEM((rows, 2 * share), BF)],
        compiler_params=params(24),
        name="out_projection",
    )(table([yl]), own, other, weight)


def angles_of(positions):
    freqs = 10000.0 ** (-(jnp.arange(HD // 2, dtype=F32) * 2.0) / HD)
    angles = positions[:, None] * freqs[None, :]
    cosine, sine = jnp.cos(angles), jnp.sin(angles)
    return jnp.concatenate([cosine, cosine], axis=1), jnp.concatenate([-sine, sine], axis=1)


def shards(
    cond_hidden,
    cond_down,
    cond_resid,
    cond_gain,
    text_proj,
    image_states,
    image_mod,
    text_mod,
    query_gain,
    key_gain,
    image_qkv,
    text_qkv,
    image_out,
    text_out,
    cond_pos,
    image_cache,
    text_cache,
):
    seq_index = lax.axis_index(SEQ)
    tp_index = lax.axis_index(TP)
    image_rows, share = image_states.shape
    text_rows = cond_hidden.shape[0]

    yh, z, c, x, yl = (lax.axis_index(a) for a in AXES)
    together = lax.optimization_barrier
    outs = jnp.stack([jnp.transpose(image_out), jnp.transpose(text_out)])
    weight = jnp.transpose(jnp.concatenate([image_qkv, text_qkv], axis=1), (1, 0, 2))

    a_pair = shift(image_states, "yl", 1)
    a_near = near(image_states, "x")
    w_pair = shift(weight, "yh", 1)
    cond_hidden, a_pair, a_near = together((cond_hidden, a_pair, a_near))

    w_near = near(weight, "z")
    a_next = near(a_pair, "x")
    partial_value = jnp.dot(cond_hidden, cond_down, preferred_element_type=F32).astype(BF)
    enc_share = cond_down.shape[1] // 8
    sent = jnp.transpose(partial_value.reshape(text_rows, 8, enc_share), (1, 0, 2))
    got = lax.all_to_all(sent, TP, split_axis=0, concat_axis=0, tiled=True)
    got, a_near, a_next, w_near, w_pair, outs = together(
        (got, a_near, a_next, w_near, w_pair, outs)
    )

    a_far = (shift(a_near[0], "x", 1), shift(a_next[1], "x", -1))
    w_next = near(w_pair, "z")
    turned = [
        (4 * zh + 2 * zl + y, 4 * zh + 2 * y + zl)
        for zh in range(2)
        for zl in range(2)
        for y in range(2)
    ]
    outs = lax.ppermute(outs, ("z", "yl"), turned)
    out_w = lax.all_gather(outs, SEQ)
    cond_state = (jnp.sum(got.astype(F32), axis=0) + cond_resid.astype(F32)).astype(BF)
    state = spread(cond_state, TP)
    state, a_far, w_near, w_next, outs = together((state, a_far, w_near, w_next, outs))

    text_states = text_projection(state, cond_gain, text_proj)
    text_a = spread(text_states, TP)
    w_far = (shift(w_near[0], "z", 1), shift(w_next[1], "z", -1))

    blocks = [(p, d) for p in range(2) for d in (0, 3, 1, 2)]
    a_arrays = [image_states, *a_near, a_far[0], a_pair, *a_next, a_far[1]]
    a_places = [(x + d) % 4 * 2 + (yl + p) % 2 for p, d in blocks]
    image_modded = modulate(a_arrays, a_places, image_mod)
    w_early = [weight, *w_near, w_pair, *w_next]
    w_swapped = [shift(w, "c", 1) for w in w_early]
    text_a, w_far, image_modded, w_swapped = together((text_a, w_far, image_modded, w_swapped))

    w_last = [shift(w, "c", 1) for w in w_far]
    w_arrays = [weight, *w_near, w_far[0], w_pair, *w_next, w_far[1]]
    w_arrays += w_swapped[:3] + w_last[:1] + w_swapped[3:] + w_last[1:]

    gains = jnp.stack([query_gain, key_gain])
    image_pos = (seq_index * image_rows + jnp.arange(image_rows)).astype(F32)
    w_places = [
        (yh + p) % 2 * 8 + (z + d) % 4 * 2 + (c + k) % 2 for k in range(2) for p, d in blocks
    ]
    query, kv = qkv(
        image_modded,
        text_a,
        w_arrays,
        w_places,
        text_mod,
        *angles_of(jnp.concatenate([image_pos, cond_pos.astype(F32)])),
        gains,
    )
    pair_query = shift(query, "yh", 1)
    kv_left, kv_right = near(kv, "z")
    core_query = shift(query, "c", 1)
    own_queries = [query, core_query]
    own = attention(own_queries, [(kv,)])
    pair_query, own = together((pair_query, own))
    pair_queries = [pair_query, shift(pair_query, "c", 1)]
    pair = attention(pair_queries, [(kv,)])
    pair, kv_left, kv_right = together((pair, kv_left, kv_right))
    kv_far = (shift(kv_left[0], "z", 1), shift(kv_right[1], "z", -1))
    pair = attention(pair_queries, [(kv_left,), (kv_right,)], pair)
    pair, kv_far = together((pair, kv_far))
    pair = attention(pair_queries, [kv_far], pair)

    sent_num = pair[0] + shift(pair[1], "c", 1)
    sent_tot = pair[2] + shift(pair[3], "c", 1)
    high = sent_tot.astype(BF)
    low = (sent_tot - high.astype(F32)).astype(BF)
    mixed = jnp.concatenate([sent_num.astype(BF), high[:, :64], low[:, :64]], axis=1)
    mixed, own = together((mixed, own))
    back = shift(mixed, "yh", 1)
    own = attention(own_queries, [(kv_left,), (kv_right,), kv_far], own)
    back, own = together((back, own))
    attended = combine(own[0], shift(own[1], "c", 1), back, own[2], shift(own[3], "c", 1))

    parts = out_projection(attended, shift(attended, "yl", 1), out_w, yl)
    got = lax.all_to_all(parts, "x", split_axis=0, concat_axis=0, tiled=True)
    branch = jnp.sum(got.astype(F32), axis=0)

    def finish(states, mod, rows, cache):
        gates = lax.dynamic_slice_in_dim(mod, tp_index * share, share, 1)
        return (
            states.astype(F32) + gates[2] * branch[rows] + gates[3] * cache.astype(F32)
        ).astype(BF)

    return (
        finish(image_states, image_mod, slice(0, image_rows), image_cache),
        finish(text_states, text_mod, slice(image_rows, None), text_cache),
    )


def solution(mesh):
    fine = Mesh(mesh.devices.reshape(2, 4, 2, 4, 2), AXES)
    return jax.shard_map(
        shards,
        mesh=fine,
        in_specs=(
            P(SEQ, TP),
            P(TP, None),
            P(SEQ, TP),
            P(),
            P(None, TP),
            P(SEQ, TP),
            P(),
            P(),
            P(),
            P(),
            P(SEQ, None, TP),
            P(SEQ, None, TP),
            P(TP, SEQ),
            P(TP, SEQ),
            P(SEQ),
            P(SEQ, TP),
            P(SEQ, TP),
        ),
        out_specs=(P(SEQ, TP), P(SEQ, TP)),
        check_vma=False,
    )
```

```python
import functools
import math

import jax
import jax.numpy as jnp
from jax import lax
from jax.experimental import pallas as pl
from jax.experimental.pallas import tpu as pltpu
from jax.sharding import Mesh, PartitionSpec as P

EPS = 1e-06
HD = 128
AXES = ("yh", "z", "c", "x", "yl")
SEQ = ("yh", "z", "c")
TP = ("x", "yl")
BF = jnp.bfloat16
F32 = jnp.float32


def shift(value, axis, step):
    size = lax.axis_size(axis)
    return lax.ppermute(value, axis, [(k, (k + step) % size) for k in range(size)])


def near(value, axis):
    return shift(value, axis, 1), shift(value, axis, -1)


def spread(value, axes):
    count = lax.axis_size(axes)
    copies = jnp.broadcast_to(value[None], (count,) + value.shape)
    return lax.all_to_all(copies, axes, split_axis=0, concat_axis=0, tiled=True)


def table(places):
    return jnp.stack([jnp.asarray(p, jnp.int32) for p in places])


def params(mib):
    return pltpu.CompilerParams(vmem_limit_bytes=mib * 1024 * 1024)


ANY = pl.BlockSpec(memory_space=pl.ANY)
VMEM = pl.BlockSpec(memory_space=pltpu.VMEM)
SMEM = pl.BlockSpec(memory_space=pltpu.SMEM)


def text_kernel(state_ref, gain_ref, proj_ref, out_ref):
    parts, rows, share = state_ref.shape
    square = jnp.zeros((rows, 1), F32)
    for t in range(parts):
        block = state_ref[t].astype(F32)
        square += jnp.sum(block * block, axis=-1, keepdims=True)
    factor = lax.rsqrt(square / (parts * share) + EPS)
    total = jnp.zeros(out_ref.shape, F32)
    for t in range(parts):
        normed = (state_ref[t].astype(F32) * factor * gain_ref[t]).astype(BF)
        total += jnp.dot(normed, proj_ref[t], preferred_element_type=F32)
    out_ref[...] = total.astype(BF)


def text_projection(state, gain, proj):
    parts, rows, share = state.shape
    return pl.pallas_call(
        text_kernel,
        out_shape=jax.ShapeDtypeStruct((rows, proj.shape[1]), BF),
        in_specs=[VMEM] * 3,
        out_specs=VMEM,
        compiler_params=params(16),
        name="text_projection",
    )(state, gain.reshape(parts, 1, share), proj.reshape(parts, share, proj.shape[1]))


def normalise(states, mod_ref, out_ref, first):
    parts, rows, share = states.shape
    width = parts * share
    tile = 64

    @pl.loop(0, rows // tile)
    def _(step):
        here = pl.ds(pl.multiple_of(step * tile, tile), tile)
        there = pl.ds(pl.multiple_of(first + step * tile, tile), tile)
        total = jnp.zeros((tile, share), F32)
        for t in range(parts):
            total += states[t, here, :].astype(F32)
        center = jnp.sum(total, axis=-1, keepdims=True) / width
        total = jnp.zeros((tile, share), F32)
        for t in range(parts):
            shifted = states[t, here, :].astype(F32) - center
            total += shifted * shifted
        factor = lax.rsqrt(jnp.sum(total, axis=-1, keepdims=True) / width + EPS)
        for t in range(parts):
            cols = slice(t * share, (t + 1) * share)
            shifted = states[t, here, :].astype(F32) - center
            normed = shifted * factor * (1.0 + mod_ref[1:2, cols]) + mod_ref[0:1, cols]
            out_ref[there, cols] = normed.astype(BF)


def modulate_kernel(count, place_ref, mod_ref, *refs):
    pieces, (out_ref, states, sems) = refs[:count], refs[count:]
    copies = [
        pltpu.make_async_copy(piece, states.at[place_ref[i]], sems.at[i])
        for i, piece in enumerate(pieces)
    ]
    for copy in copies:
        copy.start()
    for copy in copies:
        copy.wait()
    normalise(states, mod_ref, out_ref, 0)


def modulate(pieces, places, mod):
    rows, share = pieces[0].shape
    count = len(pieces)
    return pl.pallas_call(
        functools.partial(modulate_kernel, count),
        out_shape=jax.ShapeDtypeStruct((rows, count * share), BF),
        in_specs=[SMEM, VMEM] + [ANY] * count,
        out_specs=VMEM,
        scratch_shapes=[
            pltpu.VMEM((count, rows, share), BF),
            pltpu.SemaphoreType.DMA((count,)),
        ],
        compiler_params=params(16),
        name="modulate",
    )(table(places), mod, *pieces)


def qkv_kernel(count, place_ref, mod_ref, cos_ref, sin_ref, gain_ref, image_ref, *refs):
    text_ref, w_pieces, refs = refs[0], refs[1 : 1 + count], refs[1 + count :]
    q_ref, kv_ref, states, modded, weight, sems = refs
    share = states.shape[2]
    rows, width = modded.shape
    depth = width // 16
    image_rows = image_ref.shape[0]
    image_copy = pltpu.make_async_copy(
        image_ref, modded.at[pl.ds(0, image_rows)], sems.at[2 * count]
    )
    text_copy = pltpu.make_async_copy(text_ref, states, sems.at[2 * count + 1])
    w_copies = ([], [])
    for stream in range(2):
        for i, piece in enumerate(w_pieces):
            start = pl.multiple_of(place_ref[i] * depth, depth)
            src = piece.at[pl.ds(3 * stream, 3)]
            dst = weight.at[pl.ds(3 * stream, 3), pl.ds(start, depth), :]
            sem = sems.at[count * stream + i]
            w_copies[stream].append(pltpu.make_async_copy(src, dst, sem))
    for copy in [text_copy, image_copy] + w_copies[0] + w_copies[1]:
        copy.start()
    text_copy.wait()
    normalise(states, mod_ref, modded, image_rows)

    def prepare(flat, gain, cosine, sine):
        outs = []
        for h in range(share // HD):
            head = flat[:, h * HD : (h + 1) * HD]
            meansq = jnp.mean(head * head, axis=-1, keepdims=True)
            normed = head * lax.rsqrt(meansq + EPS) * gain
            outs.append(normed * cosine + pltpu.roll(normed, HD // 2, 1) * sine)
        return jnp.concatenate(outs, axis=1)

    def project(here, stream):
        def product(j):
            return jnp.dot(modded[here, :], weight[3 * stream + j], preferred_element_type=F32)

        cosine, sine = cos_ref[here, :], sin_ref[here, :]
        q = prepare(product(0), gain_ref[0:1, :], cosine, sine)
        q_ref[here, :] = (q * (math.log2(math.e) / math.sqrt(HD))).astype(BF)
        kv_ref[0, here, :] = prepare(product(1), gain_ref[1:2, :], cosine, sine).astype(BF)
        kv_ref[1, here, :] = product(2).astype(BF)

    image_copy.wait()
    for copy in w_copies[0]:
        copy.wait()
    chunk = image_rows // 2

    @pl.loop(0, 2)
    def _(step):
        project(pl.ds(pl.multiple_of(step * chunk, chunk), chunk), 0)

    for copy in w_copies[1]:
        copy.wait()
    project(pl.ds(image_rows, rows - image_rows), 1)


def qkv(image, text_a, w_pieces, w_places, mod, cosine, sine, gains):
    parts, text_rows, share = text_a.shape
    image_rows, width = image.shape
    rows = image_rows + text_rows
    count = len(w_pieces)
    return pl.pallas_call(
        functools.partial(qkv_kernel, count),
        out_shape=(
            jax.ShapeDtypeStruct((rows, share), BF),
            jax.ShapeDtypeStruct((2, rows, share), BF),
        ),
        in_specs=[SMEM, VMEM, VMEM, VMEM, VMEM] + [ANY] * (2 + count),
        out_specs=(VMEM, VMEM),
        scratch_shapes=[
            pltpu.VMEM((parts, text_rows, share), BF),
            pltpu.VMEM((rows, width), BF),
            pltpu.VMEM((6, width, share), BF),
            pltpu.SemaphoreType.DMA((2 * count + 2,)),
        ],
        compiler_params=params(36),
        name="qkv",
    )(table(w_places), mod, cosine, sine, gains, image, text_a, *w_pieces)


def attention_kernel(nq, k_sizes, first, *refs):
    nk = len(k_sizes)
    q_refs, refs = refs[:nq], refs[nq:]
    k_refs, v_refs, refs = refs[:nk], refs[nk : 2 * nk], refs[2 * nk :]
    before, refs = ([], refs) if first else (refs[: 2 * nq], refs[2 * nq :])
    out_refs, tot_refs = refs[:nq], refs[nq : 2 * nq]
    keys, values = refs[2 * nq :]
    head = pl.program_id(0)
    at = 0
    for k_ref, v_ref, size in zip(k_refs, v_refs, k_sizes):
        keys[at : at + size, :] = k_ref[0]
        values[at : at + size, 0:HD] = v_ref[0]
        at += size

    @pl.when(head == 0)
    def _():
        values[:, HD:] = jnp.ones((values.shape[0], HD), BF)
        for i in range(nq):
            tot_refs[i][...] = jnp.zeros(tot_refs[i].shape, F32) if first else before[nq + i][...]

    rows = q_refs[0].shape[0]
    lane = lax.broadcasted_iota(jnp.int32, (rows, HD), 1)
    block = 256
    for i in range(nq):
        q = q_refs[i][...]
        total = jnp.zeros((rows, 2 * HD), F32)
        for start in range(0, keys.shape[0], block):
            stop = min(start + block, keys.shape[0])
            scores = lax.dot_general(
                q, keys[start:stop, :], (((1,), (1,)), ((), ())), preferred_element_type=F32
            )
            probs = jnp.exp2(scores).astype(BF)
            total += jnp.dot(probs, values[start:stop, :], preferred_element_type=F32)
        num = total[:, :HD]
        out_refs[i][...] = num if first else before[i][...] + num
        tot_refs[i][...] += jnp.where(lane == head, total[:, HD:], 0.0)


def attention(queries, kvs, before=()):
    rows, width = queries[0].shape
    keys = [(kv[0].reshape(-1, rows, width), 0) for kv in kvs]
    values = [(kv[-1].reshape(-1, rows, width), 2 - len(kv)) for kv in kvs]
    k_sizes = (rows,) * len(kvs)
    nq = len(queries)
    by_head = pl.BlockSpec((rows, HD), lambda h: (0, h))
    fixed = pl.BlockSpec((rows, HD), lambda h: (0, 0))
    sums = [by_head] * nq + [fixed] * nq
    inputs = nq + 2 * len(kvs)
    work = nq * rows * len(kvs) * rows * width
    return pl.pallas_call(
        functools.partial(attention_kernel, nq, k_sizes, not before),
        grid=(width // HD,),
        out_shape=[jax.ShapeDtypeStruct((rows, width), F32)] * nq
        + [jax.ShapeDtypeStruct((rows, HD), F32)] * nq,
        in_specs=[by_head] * nq
        + [
            pl.BlockSpec((1, rows, HD), functools.partial(lambda i, h: (i, 0, h), i))
            for _, i in keys + values
        ]
        + (sums if before else []),
        out_specs=sums,
        input_output_aliases={inputs + i: i for i in range(2 * nq)} if before else {},
        scratch_shapes=[
            pltpu.VMEM((sum(k_sizes), HD), BF),
            pltpu.VMEM((sum(k_sizes), 2 * HD), BF),
        ],
        compiler_params=params(24),
        cost_estimate=pl.CostEstimate(
            flops=8 * work, bytes_accessed=8 * nq * rows * width, transcendentals=work // HD
        ),
        name="attention",
    )(*queries, *[k for k, _ in keys + values], *before)


def combine_kernel(num_ref, other_ref, back_ref, tot_ref, other_tot_ref, out_ref):
    share = num_ref.shape[1]
    for h in range(share // HD):
        cols = slice(h * HD, (h + 1) * HD)
        lane, low = slice(share + h, share + h + 1), slice(share + 64 + h, share + 65 + h)
        num = num_ref[:, cols] + other_ref[:, cols] + back_ref[:, cols].astype(F32)
        tot = tot_ref[:, h : h + 1] + other_tot_ref[:, h : h + 1]
        tot += back_ref[:, lane].astype(F32) + back_ref[:, low].astype(F32)
        out_ref[:, cols] = (num / tot).astype(BF)


def combine(num, other, back, tot, other_tot):
    return pl.pallas_call(
        combine_kernel,
        out_shape=jax.ShapeDtypeStruct(num.shape, BF),
        in_specs=[VMEM] * 5,
        out_specs=VMEM,
        compiler_params=params(16),
        name="combine",
    )(num, other, back, tot, other_tot)


def out_kernel(place_ref, own_ref, other_ref, weight_ref, out_ref, attended):
    rows, share = own_ref.shape
    image_rows = rows // 5 * 4

    @pl.when(pl.program_id(0) == 0)
    def _():
        first = place_ref[0] == 0
        attended[:, :share] = jnp.where(first, own_ref[...], other_ref[...])
        attended[:, share:] = jnp.where(first, other_ref[...], own_ref[...])

    for stream, here in ((0, slice(0, image_rows)), (1, slice(image_rows, rows))):
        halves = [weight_ref[2 * y : 2 * y + 2, stream].reshape(share, share) for y in range(2)]
        out_ref[0, here, :] = lax.dot_general(
            attended[here, :],
            jnp.concatenate(halves, axis=1),
            (((1,), (1,)), ((), ())),
            preferred_element_type=F32,
        ).astype(BF)


def out_projection(own, other, weight, yl):
    rows, share = own.shape
    whole = pl.BlockSpec((rows, share), lambda x: (0, 0))
    return pl.pallas_call(
        out_kernel,
        grid=(4,),
        out_shape=jax.ShapeDtypeStruct((4, rows, share), BF),
        in_specs=[SMEM, whole, whole]
        + [pl.BlockSpec((4,) + weight.shape[1:], lambda x: (x, 0, 0, 0))],
        out_specs=pl.BlockSpec((1, rows, share), lambda x: (x, 0, 0)),
        scratch_shapes=[pltpu.VMEM((rows, 2 * share), BF)],
        compiler_params=params(24),
        name="out_projection",
    )(table([yl]), own, other, weight)


def angles_of(positions):
    freqs = 10000.0 ** (-(jnp.arange(HD // 2, dtype=F32) * 2.0) / HD)
    angles = positions[:, None] * freqs[None, :]
    cosine, sine = jnp.cos(angles), jnp.sin(angles)
    return jnp.concatenate([cosine, cosine], axis=1), jnp.concatenate([-sine, sine], axis=1)


def shards(
    cond_hidden,
    cond_down,
    cond_resid,
    cond_gain,
    text_proj,
    image_states,
    image_mod,
    text_mod,
    query_gain,
    key_gain,
    image_qkv,
    text_qkv,
    image_out,
    text_out,
    cond_pos,
    image_cache,
    text_cache,
):
    seq_index = lax.axis_index(SEQ)
    tp_index = lax.axis_index(TP)
    image_rows, share = image_states.shape
    text_rows = cond_hidden.shape[0]

    yh, z, c, x, yl = (lax.axis_index(a) for a in AXES)
    together = lax.optimization_barrier
    outs = jnp.stack([jnp.transpose(image_out), jnp.transpose(text_out)])
    weight = jnp.transpose(jnp.concatenate([image_qkv, text_qkv], axis=1), (1, 0, 2))

    a_pair = shift(image_states, "yl", 1)
    a_near = near(image_states, "x")
    w_pair = shift(weight, "yh", 1)
    cond_hidden, a_pair, a_near = together((cond_hidden, a_pair, a_near))

    w_near = near(weight, "z")
    a_next = near(a_pair, "x")
    partial_value = jnp.dot(cond_hidden, cond_down, preferred_element_type=F32).astype(BF)
    enc_share = cond_down.shape[1] // 8
    sent = jnp.transpose(partial_value.reshape(text_rows, 8, enc_share), (1, 0, 2))
    got = lax.all_to_all(sent, TP, split_axis=0, concat_axis=0, tiled=True)
    got, a_near, a_next, w_near, w_pair, outs = together(
        (got, a_near, a_next, w_near, w_pair, outs)
    )

    a_far = (shift(a_near[0], "x", 1), shift(a_next[1], "x", -1))
    w_next = near(w_pair, "z")
    turned = [
        (4 * zh + 2 * zl + y, 4 * zh + 2 * y + zl)
        for zh in range(2)
        for zl in range(2)
        for y in range(2)
    ]
    outs = lax.ppermute(outs, ("z", "yl"), turned)
    out_w = lax.all_gather(outs, SEQ)
    cond_state = (jnp.sum(got.astype(F32), axis=0) + cond_resid.astype(F32)).astype(BF)
    state = spread(cond_state, TP)
    state, a_far, w_near, w_next, outs = together((state, a_far, w_near, w_next, outs))

    text_states = text_projection(state, cond_gain, text_proj)
    text_a = spread(text_states, TP)
    w_far = (shift(w_near[0], "z", 1), shift(w_next[1], "z", -1))

    blocks = [(p, d) for p in range(2) for d in (0, 3, 1, 2)]
    a_arrays = [image_states, *a_near, a_far[0], a_pair, *a_next, a_far[1]]
    a_places = [(x + d) % 4 * 2 + (yl + p) % 2 for p, d in blocks]
    image_modded = modulate(a_arrays, a_places, image_mod)
    w_early = [weight, *w_near, w_pair, *w_next]
    w_early, text_states = together((w_early, text_states))
    w_swapped = [shift(w, "c", 1) for w in w_early]
    text_a, w_far, image_modded, w_swapped = together((text_a, w_far, image_modded, w_swapped))

    w_last = [shift(w, "c", 1) for w in w_far]
    w_arrays = [weight, *w_near, w_far[0], w_pair, *w_next, w_far[1]]
    w_arrays += w_swapped[:3] + w_last[:1] + w_swapped[3:] + w_last[1:]

    gains = jnp.stack([query_gain, key_gain])
    image_pos = (seq_index * image_rows + jnp.arange(image_rows)).astype(F32)
    w_places = [
        (yh + p) % 2 * 8 + (z + d) % 4 * 2 + (c + k) % 2 for k in range(2) for p, d in blocks
    ]
    query, kv = qkv(
        image_modded,
        text_a,
        w_arrays,
        w_places,
        text_mod,
        *angles_of(jnp.concatenate([image_pos, cond_pos.astype(F32)])),
        gains,
    )
    pair_query = shift(query, "yh", 1)
    kv_left, kv_right = near(kv, "z")
    core_query = shift(query, "c", 1)
    own_queries = [query, core_query]
    own = attention(own_queries, [(kv,)])
    pair_query, own = together((pair_query, own))
    pair_queries = [pair_query, shift(pair_query, "c", 1)]
    pair = attention(pair_queries, [(kv,)])
    pair, kv_left, kv_right = together((pair, kv_left, kv_right))
    kv_far = (shift(kv_left[0], "z", 1), shift(kv_right[1], "z", -1))
    pair = attention(pair_queries, [(kv_left,), (kv_right,)], pair)
    pair, kv_far = together((pair, kv_far))
    pair = attention(pair_queries, [kv_far], pair)

    sent_num = pair[0] + shift(pair[1], "c", 1)
    sent_tot = pair[2] + shift(pair[3], "c", 1)
    high = sent_tot.astype(BF)
    low = (sent_tot - high.astype(F32)).astype(BF)
    mixed = jnp.concatenate([sent_num.astype(BF), high[:, :64], low[:, :64]], axis=1)
    mixed, own = together((mixed, own))
    back = shift(mixed, "yh", 1)
    own = attention(own_queries, [(kv_left,), (kv_right,), kv_far], own)
    back, own = together((back, own))
    attended = combine(own[0], shift(own[1], "c", 1), back, own[2], shift(own[3], "c", 1))

    parts = out_projection(attended, shift(attended, "yl", 1), out_w, yl)
    got = lax.all_to_all(parts, "x", split_axis=0, concat_axis=0, tiled=True)
    branch = jnp.sum(got.astype(F32), axis=0)

    def finish(states, mod, rows, cache):
        gates = lax.dynamic_slice_in_dim(mod, tp_index * share, share, 1)
        return (
            states.astype(F32) + gates[2] * branch[rows] + gates[3] * cache.astype(F32)
        ).astype(BF)

    return (
        finish(image_states, image_mod, slice(0, image_rows), image_cache),
        finish(text_states, text_mod, slice(image_rows, None), text_cache),
    )


def solution(mesh):
    fine = Mesh(mesh.devices.reshape(2, 4, 2, 4, 2), AXES)
    return jax.shard_map(
        shards,
        mesh=fine,
        in_specs=(
            P(SEQ, TP),
            P(TP, None),
            P(SEQ, TP),
            P(),
            P(None, TP),
            P(SEQ, TP),
            P(),
            P(),
            P(),
            P(),
            P(SEQ, None, TP),
            P(SEQ, None, TP),
            P(TP, SEQ),
            P(TP, SEQ),
            P(SEQ),
            P(SEQ, TP),
            P(SEQ, TP),
        ),
        out_specs=(P(SEQ, TP), P(SEQ, TP)),
        check_vma=False,
    )
```
